256 devices in a mesh: section: 4 (over x), blk: 32 (over y_lo, z, core), tp: 2 (over y_hi).
Axes of the slice: x: 4, y: 4 (y_hi: 2, y_lo: 2; y = y_hi * 2 + y_lo), z: 8, core: 2. Of those that a mesh axis runs over, the one named last changes fastest.
Arguments:
- patches: bfloat16 [4, 8192, 1280], P('section', 'blk'), may hold values from -8 to 8
- frame_ids: int32 [4, 8192], P('section'), may hold values from 0 to 3, never falling along the last dimension, each value on 1 to 4096 neighbouring positions
- groups: int32 [4, 2048, 4], P('section', 'blk'), may hold values from 0 to 255, as said below
- norm_gain: float32 [1280], replicated, may hold values from 0.25 to 1.75
- qkv_weight: bfloat16 [3, 1280, 1280], P(None, 'section', 'tp'), may hold values from -1 to 1
- out_weight: bfloat16 [1280, 1280], P('tp', 'section'), may hold values from -0.47851562 to 0.47851562
- merge_gain: float32 [1280], replicated, may hold values from 0.25 to 1.75
- merger_up: bfloat16 [5120, 2560], P(None, ('section', 'tp')), may hold values from -0.078125 to 0.078125
- merger_down: bfloat16 [2560, 3584], P(('section', 'tp')), may hold values from -0.125 to 0.125
Outputs:
- llm_input: bfloat16 [4, 2048, 3584], P('section', ('blk', 'tp'))
The draws below stay inside these ranges and needn't reach their ends.
Inputs may be any that keep to these rules, and one draw needn't show every extreme that they name: `groups`: each aligned block of 64 rows of a video names every patch of its device block of 256 patches exactly once. `frame_ids`: frame blocks are runs of consecutive patches, numbered upward.
All inputs are finite; a program needn't handle non-finite values.
Results may differ from the reference program's by a relative error of at most 0.024.
Values may be sent and summed in bfloat16 or wider, within the bound.
No kernel may reach another device: no remote copies, remote signals or barrier semaphores. Data moves between devices by JAX's collectives and lax.ppermute only.
A program may use at most 128 MiB of HBM per device.

```python
import math
import jax
import jax.numpy as jnp
import numpy as np
from jax import lax

D = 1280
HEADS = 16
OUT = 3584
MH = 2560
P_DEV = 256
HD = 80
NP = 8192
NM = 2048
VIDEOS = 4


def shared_direction(key):
    base = jax.random.fold_in(key, 7001)
    key_dir, key_sign = jax.random.split(base)
    direction = jnp.clip(jax.random.normal(key_dir, (D,), jnp.float32), -4.0, 4.0)
    signs = jnp.where(jax.random.bernoulli(key_sign, 0.5, (D,)), 1.0, -1.0).astype(jnp.float32)
    return (direction, signs)


def draw_patches(key, part):
    direction, signs = shared_direction(key)
    key_base, key_pick, key_strength = jax.random.split(jax.random.fold_in(key, 11), 3)
    drawn = jnp.clip(jax.random.normal(key_base, (VIDEOS, NP, D), jnp.float32), -6.0, 6.0)
    share = max(1.0 / 64.0, 4.0 / NP)
    picked = jax.random.uniform(key_pick, (VIDEOS, NP, 1), jnp.float32) < share
    strength = jax.random.uniform(key_strength, (VIDEOS, NP, 1), jnp.float32, 0.75, 1.0)
    planted = strength * direction[None, None, :] + jnp.sqrt(1.0 - strength * strength) * drawn
    result = jnp.where(picked, planted, drawn)
    return jnp.clip(result, -8.0, 8.0).astype(jnp.bfloat16)


def draw_qkv_weight(key, part):
    direction, signs = shared_direction(key)
    noise = jnp.clip(0.045 * jax.random.normal(jax.random.fold_in(key, 13), (3, D, D), jnp.float32), -0.27, 0.27)
    alpha = math.sqrt(300.0 / (D * math.sqrt(HD)))
    plant = alpha * (direction / math.sqrt(D))[:, None] * signs[None, :]
    stacked = jnp.stack([plant, plant, jnp.zeros_like(plant)], axis=0)
    return jnp.clip(noise + stacked, -1.0, 1.0).astype(jnp.bfloat16)


def draw_groups(key, part):
    blocks = NP // P_DEV
    keys = jax.random.split(key, VIDEOS * blocks)
    perms = jax.vmap(lambda single: jax.random.permutation(single, P_DEV))(keys)
    return perms.reshape(VIDEOS, NM, 4).astype(jnp.int32)


def levels(stream_key, dims, cuts, smallest, top_value):
    level = 1.0
    for dim, parts in cuts:
        steps = jax.random.uniform(jax.random.fold_in(jax.random.fold_in(stream_key, 6), dim), (parts,), jnp.float32, smallest / len(cuts), top_value / len(cuts))
        level = level * jnp.repeat(jnp.exp(steps), dims[dim] // parts).reshape((-1,) + (1,) * (len(dims) - 1 - dim))
    return level


def length_profile(number_of, total, reach, slope):
    loads = [(1 << 20) // math.isqrt(standing ** slope) + 1 for standing in range(2, number_of + 1)]
    rest, holding = total - reach - (number_of - 1), [1] * (number_of - 1)
    while rest > 0:
        movable = [i for i in range(number_of - 1) if holding[i] < reach]
        whole, budget = sum([loads[i] for i in movable]), rest
        for i in movable:
            addition = min(reach - holding[i], max(1, budget * loads[i] // whole), rest)
            holding[i] = holding[i] + addition
            rest = rest - addition
    return np.array([reach] + holding)


def ragged_sizes(key, amount, total, bound, lean):
    if amount == 2:
        one = jax.random.randint(key, (), max(1, total - bound), min(bound, total - 1) + 1)
        return jnp.stack([one, total - one])
    sizes = jnp.asarray(length_profile(amount, total, bound, lean), jnp.int32)
    pairs = (amount - 1) // 2
    giver, taker = sizes[1:1 + 2 * pairs:2], sizes[2:2 + 2 * pairs:2]
    margin = jnp.minimum(giver - 1, bound - taker)
    moved = jax.random.randint(jax.random.fold_in(key, 1), (pairs,), 0, 1 << 20) % (margin + 1)
    sizes = sizes.at[1:1 + 2 * pairs:2].set(giver - moved).at[2:2 + 2 * pairs:2].set(taker + moved)
    return sizes[jax.random.permutation(jax.random.fold_in(key, 2), amount)]


def bell_draw(own_key, extent, scale, reach, cuts=(), held_as=jnp.bfloat16):
    level = levels(own_key, extent, cuts, -0.22, 0.18) if cuts else 1.0
    entries = jax.random.normal(own_key, extent, jnp.float32) * scale * level
    return jnp.minimum(jnp.maximum(entries, -reach), reach).astype(held_as)


def setup_inputs(seed: int = 0) -> dict:
    seeds = jax.random.split(jax.random.key(seed), 10)
    patches = draw_patches(jax.random.fold_in(seeds[9], 71), 0)
    frame_ids = jax.vmap(lambda own: jnp.searchsorted(jnp.cumsum(ragged_sizes(own, 4, NP, NP // 2, 0)), jnp.arange(NP), side="right"))(jax.random.split(seeds[1], VIDEOS)).reshape((VIDEOS, NP)).astype(jnp.int32)
    groups = draw_groups(jax.random.fold_in(seeds[9], 71), 0)
    norm_gain = jnp.clip(1.0 + 0.15 * jax.random.normal(seeds[3], (D,), jnp.float32), 0.25, 1.75)
    qkv_weight = draw_qkv_weight(jax.random.fold_in(seeds[9], 71), 0)
    out_weight = bell_draw(seeds[5], (D, D), 0.08, 0.47851562, ((0, 2), (1, 4)))
    merge_gain = jnp.clip(1.0 + 0.15 * jax.random.normal(seeds[6], (D,), jnp.float32), 0.25, 1.75)
    merger_up = bell_draw(seeds[7], (4 * D, MH), (4 * D) ** -0.5, 0.078125, ((1, 8),))
    merger_down = bell_draw(seeds[8], (MH, OUT), MH ** -0.5, 0.125, ((0, 8),))
    return {"patches": patches, "frame_ids": frame_ids, "groups": groups, "norm_gain": norm_gain, "qkv_weight": qkv_weight, "out_weight": out_weight, "merge_gain": merge_gain, "merger_up": merger_up, "merger_down": merger_down}


def rms_norm(value, gain):
    return value * lax.rsqrt(lax.optimization_barrier(jnp.mean(value * value, axis=-1, keepdims=True)) + 1e-06) * gain

def one_head(args):
    query, keys, values, frames = args
    scores = jnp.dot(query, keys.T, preferred_element_type=jnp.float32) * HD ** (-0.5)
    visible = frames[:, None] == frames[None, :]
    scores = jnp.where(visible, scores, -1e+30)
    top = lax.optimization_barrier(jnp.max(scores, axis=-1, keepdims=True))
    weights = jnp.where(visible, jnp.exp(scores - top), 0.0)
    total = lax.optimization_barrier(jnp.sum(weights, axis=-1, keepdims=True))
    out = jnp.dot(weights.astype(jnp.bfloat16), values, preferred_element_type=jnp.float32) / total
    return out.astype(jnp.bfloat16)

def reference(patches, frame_ids, groups, norm_gain, qkv_weight, out_weight, merge_gain, merger_up, merger_down):

    def one_video(args):
        patch_rows, frames, group_rows = args
        xfloat = patch_rows.astype(jnp.float32)
        normed = rms_norm(xfloat, norm_gain).astype(jnp.bfloat16)
        query = jnp.dot(normed, qkv_weight[0], preferred_element_type=jnp.float32).astype(jnp.bfloat16)
        keys = jnp.dot(normed, qkv_weight[1], preferred_element_type=jnp.float32).astype(jnp.bfloat16)
        values = jnp.dot(normed, qkv_weight[2], preferred_element_type=jnp.float32).astype(jnp.bfloat16)
        query = query.reshape(NP, HEADS, HD).transpose(1, 0, 2)
        keys = keys.reshape(NP, HEADS, HD).transpose(1, 0, 2)
        values = values.reshape(NP, HEADS, HD).transpose(1, 0, 2)
        frame_rep = jnp.broadcast_to(frames, (HEADS, NP))
        attn = lax.map(one_head, (query, keys, values, frame_rep))
        attn = attn.transpose(1, 0, 2).reshape(NP, D)
        resid = xfloat + jnp.dot(attn, out_weight, preferred_element_type=jnp.float32)
        merged_normed = rms_norm(resid, merge_gain).astype(jnp.bfloat16)
        offset = jnp.arange(NM, dtype=jnp.int32) // (P_DEV // 4) * P_DEV
        index = group_rows.astype(jnp.int32) + offset[:, None]
        tokens = merged_normed[index].reshape(NM, 4 * D)
        hidden = jax.nn.gelu(jnp.dot(tokens, merger_up, preferred_element_type=jnp.float32), approximate=False).astype(jnp.bfloat16)
        return jnp.dot(hidden, merger_down, preferred_element_type=jnp.float32).astype(jnp.bfloat16)
    merged_out = lax.map(one_video, (patches, frame_ids, groups))
    return jnp.roll(merged_out, 1, axis=0)
```

```python
import functools
import math

import jax
import jax.numpy as jnp
from jax import lax
from jax.experimental import pallas as pl
from jax.experimental.pallas import tpu as pltpu
from jax.sharding import PartitionSpec as P

HD = 80
ZN = 8
KB = 512
SECTIONS = 4
VMEM = pl.BlockSpec(memory_space=pltpu.VMEM)
SMEM = pl.BlockSpec(memory_space=pltpu.SMEM)
LIMIT = 56 * 1024 * 1024
bf16, f32 = jnp.bfloat16, jnp.float32

Z_GROUPS = [[y * 16 + z * 2 + c for z in range(ZN)] for y in range(2) for c in range(2)]


def call(kernel, out_shape, specs, scratch=(), flops=0, moved=0, name=None):
    return pl.pallas_call(
        kernel,
        out_shape=out_shape,
        in_specs=specs,
        out_specs=jax.tree.map(lambda _: VMEM, out_shape),
        scratch_shapes=list(scratch),
        compiler_params=pltpu.CompilerParams(vmem_limit_bytes=LIMIT),
        cost_estimate=pl.CostEstimate(flops=flops, bytes_accessed=moved, transcendentals=0),
        name=name,
    )


def section_shift(value, distance):
    route = [(i, (i + distance) % SECTIONS) for i in range(SECTIONS)]
    return lax.ppermute(value, "section", route)


def blk_swap(value, bit):
    return lax.ppermute(value, "blk", [(i, i ^ bit) for i in range(32)])


def tp_swap(value):
    return lax.ppermute(value, "tp", [(0, 1), (1, 0)])


def z_exchange(value):
    return lax.all_to_all(value, "blk", 0, 0, axis_index_groups=Z_GROUPS, tiled=True)


def rms_norm(value, gain):
    return value * lax.rsqrt(jnp.mean(value * value, axis=-1, keepdims=True) + 1e-06) * gain


def ring_halves(own):
    half = own.shape[-2] // 2
    right = section_shift(own, -1)
    left = section_shift(own, 1)
    opposite_a = section_shift(right[..., :half, :], -1)
    opposite_b = section_shift(left[..., half:, :], 1)
    return right, left, opposite_a, opposite_b


def project_kernel(count, place_ref, normed_ref, own_ref, mine_ref, other_ref, out_ref, weight):
    me, core = place_ref[0], place_ref[1]
    row = lambda section, half: pl.ds(pl.multiple_of(section * 320 + half * 160, 16), 160)
    for t in range(count):
        weight[t, pl.ds(pl.multiple_of(me * 320, 16), 320), :] = own_ref[t]
        for source, half in ((mine_ref, core), (other_ref, 1 - core)):
            for k in range(3):
                section = lax.rem(me + k + 1, SECTIONS)
                weight[t, row(section, half), :] = source[k, t]
        made = jnp.dot(normed_ref[...], weight[t], preferred_element_type=f32)
        turned = made.T.astype(bf16)
        for h in range(ZN):
            out_ref[h, t * HD : (t + 1) * HD, :] = turned[h * HD : (h + 1) * HD, :]


def project(place, normed, own, core):
    count = own.shape[0]
    half = lax.dynamic_slice_in_dim(own, core * 160, 160, axis=1)
    right, left, opp_a, opp_b = ring_halves(half)
    mine = jnp.stack([right, jnp.concatenate([opp_a, opp_b], axis=1), left])
    other = blk_swap(mine, 1)
    return call(
        functools.partial(project_kernel, count),
        jax.ShapeDtypeStruct((ZN, count * HD, 256), bf16),
        [SMEM] + [VMEM] * 4,
        [pltpu.VMEM((count, 1280, 640), bf16)],
        flops=2 * 256 * 1280 * 640 * count,
        moved=count * 2 * 1280 * 640,
        name="project",
    )(place, normed, own, mine, other)


def attention_kernel(bounds_ref, place_ref, qframe_ref, kframe_ref, q_ref, kv_ref, out_ref, keys, values):
    y, core = place_ref[2], place_ref[1]
    scale = HD ** (-0.5) * math.log2(math.e)
    filler = (lax.broadcasted_iota(jnp.int32, (48, 256), 0) == 0).astype(f32).astype(bf16)

    def arrange(step, carry):
        which, z = step // ZN, lax.rem(step, ZN)
        y_of = jnp.bitwise_xor(y, which // 2)
        core_of = jnp.bitwise_xor(core, lax.rem(which, 2))
        place = pl.multiple_of((y_of * 16 + z * 2 + core_of) * 256, 256)
        keys[:, pl.ds(place, 256)] = kv_ref[which, z, :HD, :]
        padded = jnp.concatenate([kv_ref[which, z, HD:, :], filler], axis=0)
        values[pl.ds(place, 256), :] = padded.T
        return carry

    lax.fori_loop(0, 4 * ZN, arrange, 0)

    def one_block(block, unused):
        query = q_ref[block].T
        qframe = qframe_ref[block]

        def step(masked, index, carry):
            top, accum = carry
            start = pl.multiple_of(index * KB, KB)
            scores = jnp.dot(query, keys[:, pl.ds(start, KB)], preferred_element_type=f32)
            if masked:
                scores = jnp.where(qframe == kframe_ref[:, pl.ds(start, KB)], scores, -1e30)
            new_top = jnp.maximum(top, jnp.max(scores, axis=1, keepdims=True))
            weights = jnp.exp2((scores - new_top) * scale)
            factor = jnp.exp2((top - new_top) * scale)
            product = jnp.dot(weights.astype(bf16), values[pl.ds(start, KB), :], preferred_element_type=f32)
            return new_top, accum * factor + product

        first, inner, outer, last = (bounds_ref[k, block] for k in range(4))
        carry = (jnp.full((256, 1), -1e30, f32), jnp.zeros((256, 128), f32))
        carry = lax.fori_loop(first, inner, functools.partial(step, True), carry)
        carry = lax.fori_loop(inner, outer, functools.partial(step, False), carry)
        carry = lax.fori_loop(outer, last, functools.partial(step, True), carry)
        accum = carry[1]
        result = accum / accum[:, HD : HD + 1]
        out_ref[block] = result.T[:HD, :].astype(bf16)
        return unused

    lax.fori_loop(0, ZN, one_block, 0)


def attention(place, frames, q, kv, y, core):
    ends = jnp.sum((frames[None, :] <= jnp.arange(-1, 4)[:, None]).astype(jnp.int32), axis=1)
    grid = frames.reshape(2, ZN, 2, 256)
    mine = lax.dynamic_index_in_dim(lax.dynamic_index_in_dim(grid, y, 0, False), core, 1, False)
    low, high = mine[:, 0], mine[:, -1]
    start, stop = ends[low], ends[high + 1]
    single = low == high
    first, last = start // KB, (stop + KB - 1) // KB
    inner = jnp.where(single, (start + KB - 1) // KB, last)
    outer = jnp.where(single, stop // KB, last)
    inner = jnp.minimum(inner, last)
    outer = jnp.maximum(outer, inner)
    bounds = jnp.stack([first, inner, outer, last]).astype(jnp.int32)
    return call(
        attention_kernel,
        jax.ShapeDtypeStruct((ZN, HD, 256), bf16),
        [SMEM, SMEM] + [VMEM] * 4,
        [pltpu.VMEM((HD, 8192), bf16), pltpu.VMEM((8192, 128), bf16)],
        flops=4 * 2048 * 4096 * 256,
        moved=4 * 8192 * HD,
        name="attention",
    )(bounds, place, mine[:, :, None], frames[None, :], q, kv)


def output_kernel(place_ref, order_ref, patch_ref, attn_ref, weight_ref, base_ref, send_ref):
    tp = place_ref[3]
    pick = (order_ref[...] == lax.broadcasted_iota(jnp.int32, (256, 256), 1)).astype(f32).astype(bf16)
    attn = attn_ref[...].reshape(ZN * HD, 256)
    picked = lax.dot_general(pick, attn, (((1,), (1,)), ((), ())), preferred_element_type=f32).astype(bf16)
    partial = jnp.dot(picked, weight_ref[...], preferred_element_type=f32)
    patch = jnp.dot(pick, patch_ref[...], preferred_element_type=f32)

    @pl.when(tp == 0)
    def _():
        base_ref[...] = partial[:128] + patch[:128]
        send_ref[...] = partial[128:].astype(bf16)

    @pl.when(tp == 1)
    def _():
        base_ref[...] = partial[128:] + patch[128:]
        send_ref[...] = partial[:128].astype(bf16)


def merger_kernel(place_ref, *refs):
    pieces, (up_ref, down_ref, out_ref, tokens) = refs[:10], refs[10:]
    me, tp = place_ref[0], place_ref[3]
    own, own_t, right, left, opp_a, opp_b, right_t, left_t, opp_at, opp_bt = pieces

    def put(distance, flip, source, low):
        slot = lax.rem(me + distance + 1, SECTIONS) * 2 + (1 - tp if flip else tp)
        rows = pl.ds(pl.multiple_of(slot * 32, 32), 32)
        for j in range(source.shape[0] // 32):
            tokens[low // 32 + j, rows, :] = source[j * 32 : (j + 1) * 32, :]

    put(0, False, own, 0)
    put(0, True, own_t, 0)
    put(1, False, right, 0)
    put(1, True, right_t, 0)
    put(3, False, left, 0)
    put(3, True, left_t, 0)
    put(2, False, opp_a, 0)
    put(2, False, opp_b, 64)
    put(2, True, opp_at, 0)
    put(2, True, opp_bt, 64)
    hidden = jnp.zeros((256, 320), f32)
    for j in range(4):
        hidden += jnp.dot(tokens[j], up_ref[j * 1280 : (j + 1) * 1280, :], preferred_element_type=f32)
    hidden = (0.5 * hidden * (1.0 + lax.erf(hidden * (0.5**0.5)))).astype(bf16)
    for k in range(7):
        columns = slice(k * 512, (k + 1) * 512)
        out_ref[:, columns] = jnp.dot(hidden, down_ref[:, columns], preferred_element_type=f32).astype(bf16)


def on_device(patches, frame_ids, groups, norm_gain, qkv_weight, out_weight, merge_gain, merger_up, merger_down):
    me, blk, tp = lax.axis_index("section"), lax.axis_index("blk"), lax.axis_index("tp")
    core, y = blk % 2, blk // 16
    place = jnp.stack([me, core, y, tp]).astype(jnp.int32)
    patch = patches[0]
    normed = rms_norm(patch.astype(f32), norm_gain).astype(bf16)

    kv = z_exchange(project(place, normed, qkv_weight[1:3], core))
    q = z_exchange(project(place, normed, qkv_weight[0:1], core))

    far = blk_swap(kv, 16)
    pair = jnp.stack([kv, far])
    across = blk_swap(pair, 1)
    kv_all = jnp.stack([kv, across[0], far, across[1]])

    attn = z_exchange(attention(place, frame_ids[0], q, kv_all, y, core))

    pieces = jnp.stack([out_weight] + [section_shift(out_weight, -d) for d in (1, 2, 3)])
    turned = jnp.roll(pieces, me, axis=0)
    whole = turned.transpose(1, 0, 2).reshape(640, 1280)
    order = groups[0].reshape(2, 32, 4).transpose(0, 2, 1).reshape(256, 1)
    base, send = call(
        output_kernel,
        (jax.ShapeDtypeStruct((128, 1280), f32), jax.ShapeDtypeStruct((128, 1280), bf16)),
        [SMEM] + [VMEM] * 4,
        flops=2 * 256 * 1280 * 900,
        moved=4000000,
        name="output",
    )(place, order, patch, attn, whole)
    resid = base + tp_swap(send).astype(f32)
    own = rms_norm(resid, merge_gain).astype(bf16)

    own_t = tp_swap(own)
    right, left, opp_a, opp_b = ring_halves(own)
    right_t, left_t, opp_at, opp_bt = ring_halves(own_t)
    partial = call(
        merger_kernel,
        jax.ShapeDtypeStruct((256, 3584), bf16),
        [SMEM] + [VMEM] * 12,
        [pltpu.VMEM((4, 256, 1280), bf16)],
        flops=2 * 256 * 320 * (5120 + 3584),
        moved=9000000,
        name="merger",
    )(place, own, own_t, right, left, opp_a, opp_b, right_t, left_t, opp_at, opp_bt, merger_up, merger_down)
    parts = lax.all_to_all(partial.reshape(8, 32, 3584), ("section", "tp"), 0, 0, tiled=True)
    return jnp.sum(parts.astype(f32), axis=0).astype(bf16)[None]


def solution(mesh):
    in_specs = (
        P("section", "blk", None),
        P("section", None),
        P("section", "blk", None),
        P(),
        P(None, "section", "tp"),
        P("tp", "section"),
        P(),
        P(None, ("section", "tp")),
        P(("section", "tp"), None),
    )
    out_specs = P("section", ("blk", "tp"), None)
    return jax.shard_map(on_device, mesh=mesh, in_specs=in_specs, out_specs=out_specs, check_vma=False)
```

```python
import functools
import math

import jax
import jax.numpy as jnp
from jax import lax
from jax.experimental import pallas as pl
from jax.experimental.pallas import tpu as pltpu
from jax.sharding import PartitionSpec as P

HD = 80
ZN = 8
KB = 512
SECTIONS = 4
VMEM = pl.BlockSpec(memory_space=pltpu.VMEM)
SMEM = pl.BlockSpec(memory_space=pltpu.SMEM)
LIMIT = 56 * 1024 * 1024
bf16, f32 = jnp.bfloat16, jnp.float32

Z_GROUPS = [[y * 16 + z * 2 + c for z in range(ZN)] for y in range(2) for c in range(2)]


def call(kernel, out_shape, specs, scratch=(), flops=0, moved=0, name=None):
    return pl.pallas_call(
        kernel,
        out_shape=out_shape,
        in_specs=specs,
        out_specs=jax.tree.map(lambda _: VMEM, out_shape),
        scratch_shapes=list(scratch),
        compiler_params=pltpu.CompilerParams(vmem_limit_bytes=LIMIT),
        cost_estimate=pl.CostEstimate(flops=flops, bytes_accessed=moved, transcendentals=0),
        name=name,
    )


def section_shift(value, distance):
    route = [(i, (i + distance) % SECTIONS) for i in range(SECTIONS)]
    return lax.ppermute(value, "section", route)


def blk_swap(value, bit):
    return lax.ppermute(value, "blk", [(i, i ^ bit) for i in range(32)])


def tp_swap(value):
    return lax.ppermute(value, "tp", [(0, 1), (1, 0)])


def z_exchange(value):
    return lax.all_to_all(value, "blk", 0, 0, axis_index_groups=Z_GROUPS, tiled=True)


def rms_norm(value, gain):
    return value * lax.rsqrt(jnp.mean(value * value, axis=-1, keepdims=True) + 1e-06) * gain


def ring_halves(own):
    half = own.shape[-2] // 2
    right = section_shift(own, -1)
    left = section_shift(own, 1)
    opposite_a = section_shift(right[..., :half, :], -1)
    opposite_b = section_shift(left[..., half:, :], 1)
    return right, left, opposite_a, opposite_b


def project_kernel(scale, count, place_ref, normed_ref, own_ref, mine_ref, other_ref, out_ref, weight):
    me, core = place_ref[0], place_ref[1]
    row = lambda section, half: pl.ds(pl.multiple_of(section * 320 + half * 160, 16), 160)
    for t in range(count):
        weight[t, pl.ds(pl.multiple_of(me * 320, 16), 320), :] = own_ref[t]
        for source, half in ((mine_ref, core), (other_ref, 1 - core)):
            for k in range(3):
                section = lax.rem(me + k + 1, SECTIONS)
                weight[t, row(section, half), :] = source[k, t]
        made = jnp.dot(normed_ref[...], weight[t], preferred_element_type=f32)
        turned = (made * scale).T.astype(bf16)
        for h in range(ZN):
            out_ref[h, t * HD : (t + 1) * HD, :] = turned[h * HD : (h + 1) * HD, :]


def project(place, normed, own, core, scale):
    count = own.shape[0]
    half = lax.dynamic_slice_in_dim(own, core * 160, 160, axis=1)
    right, left, opp_a, opp_b = ring_halves(half)
    mine = jnp.stack([right, jnp.concatenate([opp_a, opp_b], axis=1), left])
    other = blk_swap(mine, 1)
    return call(
        functools.partial(project_kernel, scale, count),
        jax.ShapeDtypeStruct((ZN, count * HD, 256), bf16),
        [SMEM] + [VMEM] * 4,
        [pltpu.VMEM((count, 1280, 640), bf16)],
        flops=2 * 256 * 1280 * 640 * count,
        moved=count * 2 * 1280 * 640,
        name="project",
    )(place, normed, own, mine, other)


def attention_kernel(bounds_ref, place_ref, qframe_ref, kframe_ref, q_ref, own, near, far, across, out_ref, keys, values, held):
    y, core = place_ref[2], place_ref[1]
    filler = (lax.broadcasted_iota(jnp.int32, (48, 256), 0) == 0).astype(f32).astype(bf16)
    frame = lax.broadcasted_iota(jnp.int32, (16, 256), 0)

    def arrange(z, unused):
        for which, source in enumerate((own, near, far, across)):
            y_of = jnp.bitwise_xor(y, which // 2)
            core_of = jnp.bitwise_xor(core, which % 2)
            place = pl.ds(pl.multiple_of((y_of * 16 + z * 2 + core_of) * 256, 256), 256)
            keys[:HD, place] = source[z, :HD, :]
            other = (frame < 4) & (frame != kframe_ref[:, place])
            keys[HD:, place] = jnp.where(other, -1e30, 0.0).astype(bf16)
            values[place, :] = jnp.concatenate([source[z, HD:, :], filler], axis=0).T
        return unused

    lax.fori_loop(0, ZN, arrange, 0)

    def one_block(block, unused):
        tag = (frame == qframe_ref[pl.ds(block, 1), :]).astype(f32).astype(bf16)
        query = jnp.concatenate([q_ref[block], tag], axis=0).T
        first, last = bounds_ref[0, block], bounds_ref[1, block]

        def part(index):
            return pl.ds(pl.multiple_of(index * KB, KB), KB)

        def scores_of(index):
            return jnp.dot(query, keys[:, part(index)], preferred_element_type=f32)

        def absorb(scores, index, carry):
            top, accum = carry
            new_top = jnp.maximum(top, jnp.max(scores, axis=1, keepdims=True))
            weights = jnp.exp2(scores - new_top).astype(bf16)
            product = jnp.dot(weights, values[part(index), :], preferred_element_type=f32)
            return new_top, accum * jnp.exp2(top - new_top) + product

        def run(length, start, count, carry):
            def body(step, carry):
                index = start + length * step
                for k in range(length):
                    scores = held[k % 2]
                    held[(k + 1) % 2] = scores_of(jnp.minimum(index + k + 1, last - 1))
                    carry = absorb(scores, index + k, carry)
                return carry

            return lax.fori_loop(0, count, body, carry)

        held[0] = scores_of(first)
        carry = (jnp.full((256, 1), -1e30, f32), jnp.zeros((256, 128), f32))
        fours = (last - first) // 4
        carry = run(4, first, fours, carry)
        rest = first + 4 * fours
        twos = (last - rest) // 2
        carry = run(2, rest, twos, carry)
        carry = lax.fori_loop(rest + 2 * twos, last, lambda index, c: absorb(held[0], index, c), carry)
        accum = carry[1]
        result = accum / accum[:, HD : HD + 1]
        out_ref[block] = result.T[:HD, :].astype(bf16)
        return unused

    lax.fori_loop(0, ZN, one_block, 0)


def attention(place, frames, q, sources, y, core):
    ends = jnp.sum((frames[None, :] <= jnp.arange(-1, 4)[:, None]).astype(jnp.int32), axis=1)
    grid = frames.reshape(2, ZN, 2, 256)
    mine = lax.dynamic_index_in_dim(lax.dynamic_index_in_dim(grid, y, 0, False), core, 1, False)
    start, stop = ends[mine[:, 0]], ends[mine[:, -1] + 1]
    bounds = jnp.stack([start // KB, (stop + KB - 1) // KB]).astype(jnp.int32)
    return call(
        attention_kernel,
        jax.ShapeDtypeStruct((ZN, HD, 256), bf16),
        [SMEM, SMEM] + [VMEM] * 7,
        [pltpu.VMEM((HD + 16, 8192), bf16), pltpu.VMEM((8192, 128), bf16), pltpu.VMEM((2, 256, KB), f32)],
        flops=4 * 2048 * 4096 * 256,
        moved=4 * 8192 * HD,
        name="attention",
    )(bounds, place, mine, frames[None, :], q, *sources)


def output_kernel(place_ref, order_ref, patch_ref, attn_ref, weight_ref, base_ref, send_ref):
    tp = place_ref[3]
    pick = (order_ref[...] == lax.broadcasted_iota(jnp.int32, (256, 256), 1)).astype(f32).astype(bf16)
    attn = attn_ref[...].reshape(ZN * HD, 256)
    picked = lax.dot_general(pick, attn, (((1,), (1,)), ((), ())), preferred_element_type=f32).astype(bf16)
    partial = jnp.dot(picked, weight_ref[...], preferred_element_type=f32)
    patch = jnp.dot(pick, patch_ref[...], preferred_element_type=f32)

    @pl.when(tp == 0)
    def _():
        base_ref[...] = partial[:128] + patch[:128]
        send_ref[...] = partial[128:].astype(bf16)

    @pl.when(tp == 1)
    def _():
        base_ref[...] = partial[128:] + patch[128:]
        send_ref[...] = partial[:128].astype(bf16)


def merger_kernel(place_ref, *refs):
    pieces, (up_ref, down_ref, out_ref, tokens) = refs[:10], refs[10:]
    me, tp = place_ref[0], place_ref[3]
    own, own_t, right, left, opp_a, opp_b, right_t, left_t, opp_at, opp_bt = pieces

    def put(distance, flip, source, low):
        slot = lax.rem(me + distance + 1, SECTIONS) * 2 + (1 - tp if flip else tp)
        rows = pl.ds(pl.multiple_of(slot * 32, 32), 32)
        for j in range(source.shape[0] // 32):
            tokens[low // 32 + j, rows, :] = source[j * 32 : (j + 1) * 32, :]

    put(0, False, own, 0)
    put(0, True, own_t, 0)
    put(1, False, right, 0)
    put(1, True, right_t, 0)
    put(3, False, left, 0)
    put(3, True, left_t, 0)
    put(2, False, opp_a, 0)
    put(2, False, opp_b, 64)
    put(2, True, opp_at, 0)
    put(2, True, opp_bt, 64)
    hidden = jnp.zeros((256, 320), f32)
    for j in range(4):
        hidden += jnp.dot(tokens[j], up_ref[j * 1280 : (j + 1) * 1280, :], preferred_element_type=f32)
    hidden = (0.5 * hidden * (1.0 + lax.erf(hidden * (0.5**0.5)))).astype(bf16)
    for k in range(7):
        columns = slice(k * 512, (k + 1) * 512)
        out_ref[:, columns] = jnp.dot(hidden, down_ref[:, columns], preferred_element_type=f32).astype(bf16)


def on_device(patches, frame_ids, groups, norm_gain, qkv_weight, out_weight, merge_gain, merger_up, merger_down):
    me, blk, tp = lax.axis_index("section"), lax.axis_index("blk"), lax.axis_index("tp")
    core, y = blk % 2, blk // 16
    place = jnp.stack([me, core, y, tp]).astype(jnp.int32)
    patch = patches[0]
    normed = rms_norm(patch.astype(f32), norm_gain).astype(bf16)

    kv = z_exchange(project(place, normed, qkv_weight[1:3], core, 1.0))
    q = project(place, normed, qkv_weight[0:1], core, HD ** (-0.5) * math.log2(math.e))
    kv, q = lax.optimization_barrier((kv, q))
    far = blk_swap(kv, 16)
    near = blk_swap(kv, 1)
    q = z_exchange(q)
    across = blk_swap(far, 1)

    pieces = jnp.stack([out_weight] + [section_shift(out_weight, -d) for d in (1, 2, 3)])
    turned = jnp.roll(pieces, me, axis=0)
    whole = turned.transpose(1, 0, 2).reshape(640, 1280)
    across, whole = lax.optimization_barrier((across, whole))

    attn = z_exchange(attention(place, frame_ids[0], q, (kv, near, far, across), y, core))

    order = groups[0].reshape(2, 32, 4).transpose(0, 2, 1).reshape(256, 1)
    base, send = call(
        output_kernel,
        (jax.ShapeDtypeStruct((128, 1280), f32), jax.ShapeDtypeStruct((128, 1280), bf16)),
        [SMEM] + [VMEM] * 4,
        flops=2 * 256 * 1280 * 900,
        moved=4000000,
        name="output",
    )(place, order, patch, attn, whole)
    resid = base + tp_swap(send).astype(f32)
    own = rms_norm(resid, merge_gain).astype(bf16)

    own_t = tp_swap(own)
    right, left, opp_a, opp_b = ring_halves(own)
    right_t, left_t, opp_at, opp_bt = ring_halves(own_t)
    partial = call(
        merger_kernel,
        jax.ShapeDtypeStruct((256, 3584), bf16),
        [SMEM] + [VMEM] * 12,
        [pltpu.VMEM((4, 256, 1280), bf16)],
        flops=2 * 256 * 320 * (5120 + 3584),
        moved=9000000,
        name="merger",
    )(place, own, own_t, right, left, opp_a, opp_b, right_t, left_t, opp_at, opp_bt, merger_up, merger_down)
    parts = lax.all_to_all(partial.reshape(8, 32, 3584), ("section", "tp"), 0, 0, tiled=True)
    return jnp.sum(parts.astype(f32), axis=0).astype(bf16)[None]


def solution(mesh):
    in_specs = (
        P("section", "blk", None),
        P("section", None),
        P("section", "blk", None),
        P(),
        P(None, "section", "tp"),
        P("tp", "section"),
        P(),
        P(None, ("section", "tp")),
        P(("section", "tp"), None),
    )
    out_specs = P("section", ("blk", "tp"), None)
    return jax.shard_map(on_device, mesh=mesh, in_specs=in_specs, out_specs=out_specs, check_vma=False)
```

```python
import functools
import math

import jax
import jax.numpy as jnp
from jax import lax
from jax.experimental import pallas as pl
from jax.experimental.pallas import tpu as pltpu
from jax.sharding import PartitionSpec as P

HD = 80
ZN = 8
KB = 512
SECTIONS = 4
VMEM = pl.BlockSpec(memory_space=pltpu.VMEM)
SMEM = pl.BlockSpec(memory_space=pltpu.SMEM)
LIMIT = 56 * 1024 * 1024
bf16, f32 = jnp.bfloat16, jnp.float32

Z_GROUPS = [[y * 16 + z * 2 + c for z in range(ZN)] for y in range(2) for c in range(2)]


def call(kernel, out_shape, specs, scratch=(), flops=0, moved=0, name=None):
    return pl.pallas_call(
        kernel,
        out_shape=out_shape,
        in_specs=specs,
        out_specs=jax.tree.map(lambda _: VMEM, out_shape),
        scratch_shapes=list(scratch),
        compiler_params=pltpu.CompilerParams(vmem_limit_bytes=LIMIT),
        cost_estimate=pl.CostEstimate(flops=flops, bytes_accessed=moved, transcendentals=0),
        name=name,
    )


def section_shift(value, distance):
    route = [(i, (i + distance) % SECTIONS) for i in range(SECTIONS)]
    return lax.ppermute(value, "section", route)


def blk_swap(value, bit):
    return lax.ppermute(value, "blk", [(i, i ^ bit) for i in range(32)])


def tp_swap(value):
    return lax.ppermute(value, "tp", [(0, 1), (1, 0)])


def z_exchange(value):
    return lax.all_to_all(value, "blk", 0, 0, axis_index_groups=Z_GROUPS, tiled=True)


def rms_norm(value, gain):
    return value * lax.rsqrt(jnp.mean(value * value, axis=-1, keepdims=True) + 1e-06) * gain


def ring_halves(own):
    half = own.shape[-2] // 2
    right = section_shift(own, -1)
    left = section_shift(own, 1)
    opposite_a = section_shift(right[..., :half, :], -1)
    opposite_b = section_shift(left[..., half:, :], 1)
    return right, left, opposite_a, opposite_b


def project_kernel(scale, count, place_ref, normed_ref, own_ref, mine_ref, other_ref, out_ref, weight):
    me, core = place_ref[0], place_ref[1]
    row = lambda section, half: pl.ds(pl.multiple_of(section * 320 + half * 160, 16), 160)
    for t in range(count):
        weight[t, pl.ds(pl.multiple_of(me * 320, 16), 320), :] = own_ref[t]
        for source, half in ((mine_ref, core), (other_ref, 1 - core)):
            for k in range(3):
                section = lax.rem(me + k + 1, SECTIONS)
                weight[t, row(section, half), :] = source[k, t]
        made = jnp.dot(normed_ref[...], weight[t], preferred_element_type=f32)
        turned = (made * scale).T.astype(bf16)
        for h in range(ZN):
            out_ref[h, t * HD : (t + 1) * HD, :] = turned[h * HD : (h + 1) * HD, :]


def fetch(own, core):
    half = lax.dynamic_slice_in_dim(own, core * 160, 160, axis=1)
    right, left, opp_a, opp_b = ring_halves(half)
    return jnp.stack([right, jnp.concatenate([opp_a, opp_b], axis=1), left])


def project(place, normed, own, mine, scale):
    count = own.shape[0]
    other = blk_swap(mine, 1)
    return call(
        functools.partial(project_kernel, scale, count),
        jax.ShapeDtypeStruct((ZN, count * HD, 256), bf16),
        [SMEM] + [VMEM] * 4,
        [pltpu.VMEM((count, 1280, 640), bf16)],
        flops=2 * 256 * 1280 * 640 * count,
        moved=count * 2 * 1280 * 640,
        name="project",
    )(place, normed, own, mine, other)


def attention_kernel(bounds_ref, place_ref, qframe_ref, kframe_ref, q_ref, own, near, far, across, out_ref, keys, values, held):
    y, core = place_ref[2], place_ref[1]
    filler = (lax.broadcasted_iota(jnp.int32, (48, 256), 0) == 0).astype(f32).astype(bf16)
    frame = lax.broadcasted_iota(jnp.int32, (16, 256), 0)

    def arrange(z, unused):
        for which, source in enumerate((own, near, far, across)):
            y_of = jnp.bitwise_xor(y, which // 2)
            core_of = jnp.bitwise_xor(core, which % 2)
            place = pl.ds(pl.multiple_of((y_of * 16 + z * 2 + core_of) * 256, 256), 256)
            keys[:HD, place] = source[z, :HD, :]
            other = (frame < 4) & (frame != kframe_ref[:, place])
            keys[HD:, place] = jnp.where(other, -1e30, 0.0).astype(bf16)
            values[place, :] = jnp.concatenate([source[z, HD:, :], filler], axis=0).T
        return unused

    lax.fori_loop(0, ZN, arrange, 0)

    def one_block(block, unused):
        tag = (frame == qframe_ref[pl.ds(block, 1), :]).astype(f32).astype(bf16)
        query = jnp.concatenate([q_ref[block], tag], axis=0).T
        first, last = bounds_ref[0, block], bounds_ref[1, block]

        def part(index):
            return pl.ds(pl.multiple_of(index * KB, KB), KB)

        def scores_of(index):
            return jnp.dot(query, keys[:, part(index)], preferred_element_type=f32)

        def absorb(scores, index, carry):
            top, accum = carry
            new_top = jnp.maximum(top, jnp.max(scores, axis=1, keepdims=True))
            weights = jnp.exp2(scores - new_top).astype(bf16)
            product = jnp.dot(weights, values[part(index), :], preferred_element_type=f32)
            return new_top, accum * jnp.exp2(top - new_top) + product

        def run(length, start, count, carry):
            def body(step, carry):
                index = start + length * step
                for k in range(length):
                    scores = held[k % 2]
                    held[(k + 1) % 2] = scores_of(jnp.minimum(index + k + 1, last - 1))
                    carry = absorb(scores, index + k, carry)
                return carry

            return lax.fori_loop(0, count, body, carry)

        held[0] = scores_of(first)
        carry = (jnp.full((256, 1), -1e30, f32), jnp.zeros((256, 128), f32))
        fours = (last - first) // 4
        carry = run(4, first, fours, carry)
        rest = first + 4 * fours
        twos = (last - rest) // 2
        carry = run(2, rest, twos, carry)
        carry = lax.fori_loop(rest + 2 * twos, last, lambda index, c: absorb(held[0], index, c), carry)
        accum = carry[1]
        result = accum / accum[:, HD : HD + 1]
        out_ref[block] = result.T[:HD, :].astype(bf16)
        return unused

    lax.fori_loop(0, ZN, one_block, 0)


def attention(place, frames, q, sources, y, core):
    ends = jnp.sum((frames[None, :] <= jnp.arange(-1, 4)[:, None]).astype(jnp.int32), axis=1)
    grid = frames.reshape(2, ZN, 2, 256)
    mine = lax.dynamic_index_in_dim(lax.dynamic_index_in_dim(grid, y, 0, False), core, 1, False)
    start, stop = ends[mine[:, 0]], ends[mine[:, -1] + 1]
    bounds = jnp.stack([start // KB, (stop + KB - 1) // KB]).astype(jnp.int32)
    return call(
        attention_kernel,
        jax.ShapeDtypeStruct((ZN, HD, 256), bf16),
        [SMEM, SMEM] + [VMEM] * 7,
        [pltpu.VMEM((HD + 16, 8192), bf16), pltpu.VMEM((8192, 128), bf16), pltpu.VMEM((2, 256, KB), f32)],
        flops=4 * 2048 * 4096 * 256,
        moved=4 * 8192 * HD,
        name="attention",
    )(bounds, place, mine, frames[None, :], q, *sources)


def output_kernel(
    place_ref, order_ref, gain_ref, patch_ref, attn_ref, attn_t_ref, own, right, left, opp_a, opp_b, out_ref, blocks
):
    me = place_ref[0]
    pick = (order_ref[...] == lax.broadcasted_iota(jnp.int32, (256, 256), 1)).astype(f32).astype(bf16)
    picked = []
    for source in (attn_ref, attn_t_ref):
        attn = source[...].reshape(ZN * HD, 256)
        chosen = lax.dot_general(pick, attn, (((1,), (1,)), ((), ())), preferred_element_type=f32)
        picked.append(chosen.astype(bf16))

    def product(weight, low, high):
        return sum(jnp.dot(picked[t][:, low:high], weight[t], preferred_element_type=f32) for t in range(2))

    blocks[me] = product(own, 0, 640)
    blocks[lax.rem(me + 1, SECTIONS)] = product(right, 0, 640)
    blocks[lax.rem(me + 3, SECTIONS)] = product(left, 0, 640)
    blocks[lax.rem(me + 2, SECTIONS)] = product(opp_a, 0, 320) + product(opp_b, 320, 640)
    total = jnp.dot(pick, patch_ref[...], preferred_element_type=f32)
    total += jnp.concatenate([blocks[section] for section in range(SECTIONS)], axis=1)
    out_ref[...] = rms_norm(total, gain_ref[...]).astype(bf16)


def merger_kernel(place_ref, own, right, left, opp_a, opp_b, up_ref, down_ref, out_ref, tokens):
    me = place_ref[0]

    def put(distance, source, first_half):
        for part in range(source.shape[0] // 128):
            slot = lax.rem(me + distance + 1, SECTIONS) * 2 + first_half + part
            rows = pl.ds(pl.multiple_of(slot * 32, 32), 32)
            for j in range(4):
                low = part * 128 + j * 32
                tokens[j, rows, :] = source[low : low + 32, :]

    put(0, own, 0)
    put(1, right, 0)
    put(3, left, 0)
    put(2, opp_a, 0)
    put(2, opp_b, 1)
    hidden = jnp.zeros((256, 320), f32)
    for j in range(4):
        hidden += jnp.dot(tokens[j], up_ref[j * 1280 : (j + 1) * 1280, :], preferred_element_type=f32)
    hidden = (0.5 * hidden * (1.0 + lax.erf(hidden * (0.5**0.5)))).astype(bf16)
    for k in range(7):
        columns = slice(k * 512, (k + 1) * 512)
        out_ref[:, columns] = jnp.dot(hidden, down_ref[:, columns], preferred_element_type=f32).astype(bf16)


def on_device(patches, frame_ids, groups, norm_gain, qkv_weight, out_weight, merge_gain, merger_up, merger_down):
    me, blk = lax.axis_index("section"), lax.axis_index("blk")
    core, y = blk % 2, blk // 16
    place = jnp.stack([me, core, y]).astype(jnp.int32)
    patch = patches[0]
    normed = rms_norm(patch.astype(f32), norm_gain).astype(bf16)

    kv_own, q_own = qkv_weight[1:3], qkv_weight[0:1]
    kv_mine, out_weight_t = lax.optimization_barrier((fetch(kv_own, core), tp_swap(out_weight)))
    kv_mine, q_own = lax.optimization_barrier((kv_mine, q_own))
    kv = z_exchange(project(place, normed, kv_own, kv_mine, 1.0))
    q = project(place, normed, q_own, fetch(q_own, core), HD ** (-0.5) * math.log2(math.e))
    out_own = jnp.stack([out_weight, out_weight_t])
    q, out_own = lax.optimization_barrier((q, out_own))
    out_right, out_left = section_shift(out_own, -1), section_shift(out_own, 1)
    kv, q = lax.optimization_barrier((kv, q))
    far = blk_swap(kv, 16)
    near = blk_swap(kv, 1)
    q = z_exchange(q)
    far, q = lax.optimization_barrier((far, q))
    across = blk_swap(far, 1)

    out_right, out_left, across = lax.optimization_barrier((out_right, out_left, across))
    out_a, out_b = section_shift(out_right[:, :320], -1), section_shift(out_left[:, 320:], 1)
    attn = z_exchange(attention(place, frame_ids[0], q, (kv, near, far, across), y, core))
    attn_t = tp_swap(attn)
    order = groups[0].reshape(2, 32, 4).transpose(0, 2, 1).reshape(256, 1)
    own = call(
        output_kernel,
        jax.ShapeDtypeStruct((256, 1280), bf16),
        [SMEM] + [VMEM] * 10,
        [pltpu.VMEM((SECTIONS, 256, 320), f32)],
        flops=2 * 256 * 1280 * 1800,
        moved=5000000,
        name="output",
    )(place, order, merge_gain[None, :], patch, attn, attn_t, out_own, out_right, out_left, out_a, out_b)

    right, left, opp_a, opp_b = ring_halves(own)
    partial = call(
        merger_kernel,
        jax.ShapeDtypeStruct((256, 3584), bf16),
        [SMEM] + [VMEM] * 7,
        [pltpu.VMEM((4, 256, 1280), bf16)],
        flops=2 * 256 * 320 * (5120 + 3584),
        moved=9000000,
        name="merger",
    )(place, own, right, left, opp_a, opp_b, merger_up, merger_down)
    parts = lax.all_to_all(partial.reshape(8, 32, 3584), ("section", "tp"), 0, 0, tiled=True)
    return jnp.sum(parts.astype(f32), axis=0).astype(bf16)[None]


def solution(mesh):
    in_specs = (
        P("section", "blk", None),
        P("section", None),
        P("section", "blk", None),
        P(),
        P(None, "section", "tp"),
        P("tp", "section"),
        P(),
        P(None, ("section", "tp")),
        P(("section", "tp"), None),
    )
    out_specs = P("section", ("blk", "tp"), None)
    return jax.shard_map(on_device, mesh=mesh, in_specs=in_specs, out_specs=out_specs, check_vma=False)
```

```python
import functools
import math

import jax
import jax.numpy as jnp
from jax import lax
from jax.experimental import pallas as pl
from jax.experimental.pallas import tpu as pltpu
from jax.sharding import PartitionSpec as P

HD = 80
ZN = 8
KB = 512
SECTIONS = 4
VMEM = pl.BlockSpec(memory_space=pltpu.VMEM)
SMEM = pl.BlockSpec(memory_space=pltpu.SMEM)
LIMIT = 56 * 1024 * 1024
bf16, f32 = jnp.bfloat16, jnp.float32

Z_GROUPS = [[y * 16 + z * 2 + c for z in range(ZN)] for y in range(2) for c in range(2)]


def call(kernel, out_shape, specs, scratch=(), flops=0, moved=0, name=None):
    return pl.pallas_call(
        kernel,
        out_shape=out_shape,
        in_specs=specs,
        out_specs=jax.tree.map(lambda _: VMEM, out_shape),
        scratch_shapes=list(scratch),
        compiler_params=pltpu.CompilerParams(vmem_limit_bytes=LIMIT),
        cost_estimate=pl.CostEstimate(flops=flops, bytes_accessed=moved, transcendentals=0),
        name=name,
    )


def section_shift(value, distance):
    route = [(i, (i + distance) % SECTIONS) for i in range(SECTIONS)]
    return lax.ppermute(value, "section", route)


def blk_swap(value, bit):
    return lax.ppermute(value, "blk", [(i, i ^ bit) for i in range(32)])


def tp_swap(value):
    return lax.ppermute(value, "tp", [(0, 1), (1, 0)])


def z_exchange(value):
    return lax.all_to_all(value, "blk", 0, 0, axis_index_groups=Z_GROUPS, tiled=True)


def rms_norm(value, gain):
    return value * lax.rsqrt(jnp.mean(value * value, axis=-1, keepdims=True) + 1e-06) * gain


def ring_halves(own):
    half = own.shape[-2] // 2
    right = section_shift(own, -1)
    left = section_shift(own, 1)
    opposite_a = section_shift(right[..., :half, :], -1)
    opposite_b = section_shift(left[..., half:, :], 1)
    return right, left, opposite_a, opposite_b


def project_kernel(scale, count, place_ref, normed_ref, own_ref, mine_ref, other_ref, out_ref, weight):
    me, core = place_ref[0], place_ref[1]
    row = lambda section, half: pl.ds(pl.multiple_of(section * 320 + half * 160, 16), 160)
    for t in range(count):
        weight[t, pl.ds(pl.multiple_of(me * 320, 16), 320), :] = own_ref[t]
        for source, half in ((mine_ref, core), (other_ref, 1 - core)):
            for k in range(3):
                section = lax.rem(me + k + 1, SECTIONS)
                weight[t, row(section, half), :] = source[k, t]
        made = jnp.dot(normed_ref[...], weight[t], preferred_element_type=f32)
        turned = (made * scale).T.astype(bf16)
        for h in range(ZN):
            out_ref[h, t * HD : (t + 1) * HD, :] = turned[h * HD : (h + 1) * HD, :]


def fetch(own, core):
    half = lax.dynamic_slice_in_dim(own, core * 160, 160, axis=1)
    right, left, opp_a, opp_b = ring_halves(half)
    return jnp.stack([right, jnp.concatenate([opp_a, opp_b], axis=1), left])


def project(place, normed, own, mine, scale):
    count = own.shape[0]
    other = blk_swap(mine, 1)
    return call(
        functools.partial(project_kernel, scale, count),
        jax.ShapeDtypeStruct((ZN, count * HD, 256), bf16),
        [SMEM] + [VMEM] * 4,
        [pltpu.VMEM((count, 1280, 640), bf16)],
        flops=2 * 256 * 1280 * 640 * count,
        moved=count * 2 * 1280 * 640,
        name="project",
    )(place, normed, own, mine, other)


def attention_kernel(bounds_ref, place_ref, qframe_ref, kframe_ref, q_ref, own, near, far, across, out_ref, keys, values, held):
    y, core = place_ref[2], place_ref[1]
    filler = (lax.broadcasted_iota(jnp.int32, (48, 256), 0) == 0).astype(f32).astype(bf16)
    frame = lax.broadcasted_iota(jnp.int32, (16, 256), 0)

    def arrange(z, unused):
        for which, source in enumerate((own, near, far, across)):
            y_of = jnp.bitwise_xor(y, which // 2)
            core_of = jnp.bitwise_xor(core, which % 2)
            place = pl.ds(pl.multiple_of((y_of * 16 + z * 2 + core_of) * 256, 256), 256)
            keys[:HD, place] = source[z, :HD, :]
            other = (frame < 4) & (frame != kframe_ref[:, place])
            keys[HD:, place] = jnp.where(other, -1e30, 0.0).astype(bf16)
            values[place, :] = jnp.concatenate([source[z, HD:, :], filler], axis=0).T
        return unused

    lax.fori_loop(0, ZN, arrange, 0)

    def one_block(block, unused):
        tag = (frame == qframe_ref[pl.ds(block, 1), :]).astype(f32).astype(bf16)
        query = jnp.concatenate([q_ref[block], tag], axis=0).T
        first, last = bounds_ref[0, block], bounds_ref[1, block]

        def part(index):
            return pl.ds(pl.multiple_of(index * KB, KB), KB)

        def scores_of(index):
            return jnp.dot(query, keys[:, part(index)], preferred_element_type=f32)

        def absorb(scores, index, carry):
            top, accum = carry
            new_top = jnp.maximum(top, jnp.max(scores, axis=1, keepdims=True))
            weights = jnp.exp2(scores - new_top).astype(bf16)
            product = jnp.dot(weights, values[part(index), :], preferred_element_type=f32)
            return new_top, accum * jnp.exp2(top - new_top) + product

        def run(length, start, count, carry):
            def body(step, carry):
                index = start + length * step
                for k in range(length):
                    scores = held[k % 2]
                    held[(k + 1) % 2] = scores_of(jnp.minimum(index + k + 1, last - 1))
                    carry = absorb(scores, index + k, carry)
                return carry

            return lax.fori_loop(0, count, body, carry)

        held[0] = scores_of(first)
        carry = (jnp.full((256, 1), -1e30, f32), jnp.zeros((256, 128), f32))
        fours = (last - first) // 4
        carry = run(4, first, fours, carry)
        rest = first + 4 * fours
        twos = (last - rest) // 2
        carry = run(2, rest, twos, carry)
        carry = lax.fori_loop(rest + 2 * twos, last, lambda index, c: absorb(held[0], index, c), carry)
        accum = carry[1]
        result = accum / accum[:, HD : HD + 1]
        out_ref[block] = result.T[:HD, :].astype(bf16)
        return unused

    lax.fori_loop(0, ZN, one_block, 0)


def attention(place, frames, q, sources, y, core):
    ends = jnp.sum((frames[None, :] <= jnp.arange(-1, 4)[:, None]).astype(jnp.int32), axis=1)
    grid = frames.reshape(2, ZN, 2, 256)
    mine = lax.dynamic_index_in_dim(lax.dynamic_index_in_dim(grid, y, 0, False), core, 1, False)
    start, stop = ends[mine[:, 0]], ends[mine[:, -1] + 1]
    bounds = jnp.stack([start // KB, (stop + KB - 1) // KB]).astype(jnp.int32)
    return call(
        attention_kernel,
        jax.ShapeDtypeStruct((ZN, HD, 256), bf16),
        [SMEM, SMEM] + [VMEM] * 7,
        [pltpu.VMEM((HD + 16, 8192), bf16), pltpu.VMEM((8192, 128), bf16), pltpu.VMEM((2, 256, KB), f32)],
        flops=4 * 2048 * 4096 * 256,
        moved=4 * 8192 * HD,
        name="attention",
    )(bounds, place, mine, frames[None, :], q, *sources)


def output_kernel(
    place_ref, order_ref, gain_ref, patch_ref, attn_ref, attn_t_ref, own, right, left, opp_a, opp_b, out_ref, blocks
):
    me = place_ref[0]
    pick = (order_ref[...] == lax.broadcasted_iota(jnp.int32, (256, 256), 1)).astype(f32).astype(bf16)
    picked = []
    for source in (attn_ref, attn_t_ref):
        attn = source[...].reshape(ZN * HD, 256)
        chosen = lax.dot_general(pick, attn, (((1,), (1,)), ((), ())), preferred_element_type=f32)
        picked.append(chosen.astype(bf16))

    def product(weight, low, high):
        return sum(jnp.dot(picked[t][:, low:high], weight[t], preferred_element_type=f32) for t in range(2))

    blocks[me] = product(own, 0, 640)
    blocks[lax.rem(me + 1, SECTIONS)] = product(right, 0, 640)
    blocks[lax.rem(me + 3, SECTIONS)] = product(left, 0, 640)
    blocks[lax.rem(me + 2, SECTIONS)] = product(opp_a, 0, 320) + product(opp_b, 320, 640)
    total = jnp.dot(pick, patch_ref[...], preferred_element_type=f32)
    total += jnp.concatenate([blocks[section] for section in range(SECTIONS)], axis=1)
    out_ref[...] = rms_norm(total, gain_ref[...]).astype(bf16)


def merger_kernel(sizes, place_ref, *refs):
    count = len(sizes)
    sources, (up_ref, down_ref), outs, tokens = refs[:count], refs[count : count + 2], refs[count + 2 : -1], refs[-1]
    tp = place_ref[3]
    place = 0
    for source, size in zip(sources, sizes):
        for part in range(size // 128):
            half = jnp.bitwise_xor(tp, place % 2)
            rows = pl.ds(pl.multiple_of(place // 2 * 64 + half * 32, 32), 32)
            for j in range(4):
                low = part * 128 + j * 32
                tokens[j, rows, :] = source[low : low + 32, :]
            place += 1
    hidden = jnp.zeros((place * 32, 320), f32)
    for j in range(4):
        hidden += jnp.dot(tokens[j], up_ref[j * 1280 : (j + 1) * 1280, :], preferred_element_type=f32)
    hidden = (0.5 * hidden * (1.0 + lax.erf(hidden * (0.5**0.5)))).astype(bf16)
    for k in range(7):
        columns = slice(k * 512, (k + 1) * 512)
        made = jnp.dot(hidden, down_ref[:, columns], preferred_element_type=f32).astype(bf16)
        for n, out in enumerate(outs):
            out[:, columns] = made[n * 32 : (n + 1) * 32]


def merge(place, pieces, merger_up, merger_down, name):
    sizes = [piece.shape[0] for piece in pieces]
    total = sum(sizes) // 4
    return call(
        functools.partial(merger_kernel, sizes),
        tuple(jax.ShapeDtypeStruct((32, 3584), bf16) for _ in range(total // 32)),
        [SMEM] + [VMEM] * (len(pieces) + 2),
        [pltpu.VMEM((4, total, 1280), bf16)],
        flops=2 * 256 * 320 * (5120 + 3584),
        moved=6000000,
        name=name,
    )(place, *pieces, merger_up, merger_down)


def send(value, distance, flip):
    route = [(s * 2 + t, (s + distance) % SECTIONS * 2 + (t ^ flip)) for s in range(SECTIONS) for t in range(2)]
    return lax.ppermute(value, ("section", "tp"), route)


def on_device(patches, frame_ids, groups, norm_gain, qkv_weight, out_weight, merge_gain, merger_up, merger_down):
    me, blk, tp = lax.axis_index("section"), lax.axis_index("blk"), lax.axis_index("tp")
    core, y = blk % 2, blk // 16
    place = jnp.stack([me, core, y, tp]).astype(jnp.int32)
    patch = patches[0]
    normed = rms_norm(patch.astype(f32), norm_gain).astype(bf16)

    kv_own, q_own = qkv_weight[1:3], qkv_weight[0:1]
    kv_mine, q_own = lax.optimization_barrier((fetch(kv_own, core), q_own))
    kv = z_exchange(project(place, normed, kv_own, kv_mine, 1.0))
    q_mine, out_weight_t = lax.optimization_barrier((fetch(q_own, core), tp_swap(out_weight)))
    out_own = jnp.stack([out_weight, out_weight_t])
    out_right, out_left = section_shift(out_own, -1), section_shift(out_own, 1)
    q = project(place, normed, q_own, q_mine, HD ** (-0.5) * math.log2(math.e))
    kv, q = lax.optimization_barrier((kv, q))
    far = blk_swap(kv, 16)
    near = blk_swap(kv, 1)
    q = z_exchange(q)
    far, q, out_right, out_left = lax.optimization_barrier((far, q, out_right, out_left))
    across = blk_swap(far, 1)
    out_a, out_b = section_shift(out_right[:, :320], -1), section_shift(out_left[:, 320:], 1)

    attn = z_exchange(attention(place, frame_ids[0], q, (kv, near, far, across), y, core))
    attn_t = tp_swap(attn)
    order = groups[0].reshape(2, 32, 4).transpose(0, 2, 1).reshape(256, 1)
    own = call(
        output_kernel,
        jax.ShapeDtypeStruct((256, 1280), bf16),
        [SMEM] + [VMEM] * 10,
        [pltpu.VMEM((SECTIONS, 256, 320), f32)],
        flops=2 * 256 * 1280 * 1800,
        moved=5000000,
        name="output",
    )(place, order, merge_gain[None, :], patch, attn, attn_t, out_own, out_right, out_left, out_a, out_b)

    right, left = section_shift(own, -1), section_shift(own, 1)
    own_same, own_other = merge(place, [own], merger_up, merger_down, "merge_own")
    right, left, own_same, own_other = lax.optimization_barrier((right, left, own_same, own_other))
    opp_a, opp_b = section_shift(right[:128], -1), section_shift(left[128:], 1)
    sums = [send(own_same, 1, 0), send(own_other, 1, 1)]
    right_same, right_other, left_same, left_other = merge(
        place, [right, left], merger_up, merger_down, "merge_next"
    )
    sums += [send(right_same, 2, 0), send(right_other, 2, 1), left_same, send(left_other, 0, 1)]
    opp_same, opp_other = merge(place, [opp_a, opp_b], merger_up, merger_down, "merge_opposite")
    sums += [send(opp_same, 3, 0), send(opp_other, 3, 1)]
    return sum(part.astype(f32) for part in sums).astype(bf16)[None]


def solution(mesh):
    in_specs = (
        P("section", "blk", None),
        P("section", None),
        P("section", "blk", None),
        P(),
        P(None, "section", "tp"),
        P("tp", "section"),
        P(),
        P(None, ("section", "tp")),
        P(("section", "tp"), None),
    )
    out_specs = P("section", ("blk", "tp"), None)
    return jax.shard_map(on_device, mesh=mesh, in_specs=in_specs, out_specs=out_specs, check_vma=False)
```

```python
import functools
import math

import jax
import jax.numpy as jnp
from jax import lax
from jax.experimental import pallas as pl
from jax.experimental.pallas import tpu as pltpu
from jax.sharding import PartitionSpec as P

HD = 80
ZN = 8
KB = 512
SECTIONS = 4
VMEM = pl.BlockSpec(memory_space=pltpu.VMEM)
SMEM = pl.BlockSpec(memory_space=pltpu.SMEM)
MIB = 1024 * 1024
bf16, f32 = jnp.bfloat16, jnp.float32

Z_GROUPS = [[y * 16 + z * 2 + c for z in range(ZN)] for y in range(2) for c in range(2)]


def call(kernel, out_shape, specs, scratch=(), flops=0, moved=0, name=None, grant=14):
    return pl.pallas_call(
        kernel,
        out_shape=out_shape,
        in_specs=specs,
        out_specs=jax.tree.map(lambda _: VMEM, out_shape),
        scratch_shapes=list(scratch),
        compiler_params=pltpu.CompilerParams(vmem_limit_bytes=grant * MIB),
        cost_estimate=pl.CostEstimate(flops=flops, bytes_accessed=moved, transcendentals=0),
        name=name,
    )


def section_shift(value, distance):
    route = [(i, (i + distance) % SECTIONS) for i in range(SECTIONS)]
    return lax.ppermute(value, "section", route)


def blk_swap(value, bit):
    return lax.ppermute(value, "blk", [(i, i ^ bit) for i in range(32)])


def tp_swap(value):
    return lax.ppermute(value, "tp", [(0, 1), (1, 0)])


def z_exchange(value):
    return lax.all_to_all(value, "blk", 0, 0, axis_index_groups=Z_GROUPS, tiled=True)


def rms_norm(value, gain):
    return value * lax.rsqrt(jnp.mean(value * value, axis=-1, keepdims=True) + 1e-06) * gain


def project_kernel(scale, count, place_ref, normed_ref, own_ref, mine_ref, other_ref, out_ref, weight):
    me, core = place_ref[0], place_ref[1]
    row = lambda section, half: pl.ds(pl.multiple_of(section * 320 + half * 160, 16), 160)
    for t in range(count):
        weight[t, pl.ds(pl.multiple_of(me * 320, 16), 320), :] = own_ref[t]
        for source, half in ((mine_ref, core), (other_ref, 1 - core)):
            for k in range(3):
                section = lax.rem(me + k + 1, SECTIONS)
                weight[t, row(section, half), :] = source[k, t]
        made = jnp.dot(normed_ref[...], weight[t], preferred_element_type=f32)
        turned = (made * scale).T.astype(bf16)
        for h in range(ZN):
            out_ref[h, t * HD : (t + 1) * HD, :] = turned[h * HD : (h + 1) * HD, :]


def fetch(own, core, *beside):
    half = lax.dynamic_slice_in_dim(own, core * 160, 160, axis=1)
    right, left, *beside = lax.optimization_barrier((section_shift(half, -1), section_shift(half, 1), *beside))
    opp_a, opp_b = section_shift(right[:, :80], -1), section_shift(left[:, 80:], 1)
    return jnp.stack([right, jnp.concatenate([opp_a, opp_b], axis=1), left]), *beside


def project(place, normed, own, mine, scale):
    count = own.shape[0]
    other = blk_swap(mine, 1)
    return call(
        functools.partial(project_kernel, scale, count),
        jax.ShapeDtypeStruct((ZN, count * HD, 256), bf16),
        [SMEM] + [VMEM] * 4,
        [pltpu.VMEM((count, 1280, 640), bf16)],
        flops=2 * 256 * 1280 * 640 * count,
        moved=count * 2 * 1280 * 640,
        name="project",
    )(place, normed, own, mine, other)


def attention_kernel(bounds_ref, place_ref, qframe_ref, kframe_ref, q_ref, own, near, far, across, out_ref, keys, values, held):
    y, core = place_ref[2], place_ref[1]
    filler = (lax.broadcasted_iota(jnp.int32, (48, 256), 0) == 0).astype(f32).astype(bf16)
    frame = lax.broadcasted_iota(jnp.int32, (16, 256), 0)

    def arrange(z, unused):
        for which, source in enumerate((own, near, far, across)):
            y_of = jnp.bitwise_xor(y, which // 2)
            core_of = jnp.bitwise_xor(core, which % 2)
            place = pl.ds(pl.multiple_of((y_of * 16 + z * 2 + core_of) * 256, 256), 256)
            keys[:HD, place] = source[z, :HD, :]
            other = (frame < 4) & (frame != kframe_ref[:, place])
            keys[HD:, place] = jnp.where(other, -1e30, 0.0).astype(bf16)
            values[place, :] = jnp.concatenate([source[z, HD:, :], filler], axis=0).T
        return unused

    lax.fori_loop(0, ZN, arrange, 0)

    def one_block(block, unused):
        tag = (frame == qframe_ref[pl.ds(block, 1), :]).astype(f32).astype(bf16)
        query = jnp.concatenate([q_ref[block], tag], axis=0).T
        first, last = bounds_ref[0, block], bounds_ref[1, block]

        def part(index):
            return pl.ds(pl.multiple_of(index * KB, KB), KB)

        def scores_of(index):
            return jnp.dot(query, keys[:, part(index)], preferred_element_type=f32)

        def absorb(scores, index, carry):
            top, accum = carry
            new_top = jnp.maximum(top, jnp.max(scores, axis=1, keepdims=True))
            weights = jnp.exp2(scores - new_top).astype(bf16)
            product = jnp.dot(weights, values[part(index), :], preferred_element_type=f32)
            return new_top, accum * jnp.exp2(top - new_top) + product

        def run(length, start, count, carry):
            def body(step, carry):
                index = start + length * step
                for k in range(length):
                    scores = held[k % 2]
                    held[(k + 1) % 2] = scores_of(jnp.minimum(index + k + 1, last - 1))
                    carry = absorb(scores, index + k, carry)
                return carry

            return lax.fori_loop(0, count, body, carry)

        held[0] = scores_of(first)
        carry = (jnp.full((256, 1), -1e30, f32), jnp.zeros((256, 128), f32))
        fours = (last - first) // 4
        carry = run(4, first, fours, carry)
        rest = first + 4 * fours
        twos = (last - rest) // 2
        carry = run(2, rest, twos, carry)
        carry = lax.fori_loop(rest + 2 * twos, last, lambda index, c: absorb(held[0], index, c), carry)
        accum = carry[1]
        result = accum / accum[:, HD : HD + 1]
        out_ref[block] = result.T[:HD, :].astype(bf16)
        return unused

    lax.fori_loop(0, ZN, one_block, 0)


def attention(place, frames, q, sources, y, core):
    ends = jnp.sum((frames[None, :] <= jnp.arange(-1, 4)[:, None]).astype(jnp.int32), axis=1)
    grid = frames.reshape(2, ZN, 2, 256)
    mine = lax.dynamic_index_in_dim(lax.dynamic_index_in_dim(grid, y, 0, False), core, 1, False)
    start, stop = ends[mine[:, 0]], ends[mine[:, -1] + 1]
    bounds = jnp.stack([start // KB, (stop + KB - 1) // KB]).astype(jnp.int32)
    return call(
        attention_kernel,
        jax.ShapeDtypeStruct((ZN, HD, 256), bf16),
        [SMEM, SMEM] + [VMEM] * 7,
        [pltpu.VMEM((HD + 16, 8192), bf16), pltpu.VMEM((8192, 128), bf16), pltpu.VMEM((2, 256, KB), f32)],
        flops=4 * 2048 * 4096 * 256,
        moved=4 * 8192 * HD,
        name="attention",
    )(bounds, place, mine, frames[None, :], q, *sources)


def output_kernel(
    place_ref, order_ref, gain_ref, patch_ref, attn_ref, attn_t_ref, own, right, left, opp_a, opp_b, out_ref, blocks
):
    me = place_ref[0]
    pick = (order_ref[...] == lax.broadcasted_iota(jnp.int32, (256, 256), 1)).astype(f32).astype(bf16)
    picked = []
    for source in (attn_ref, attn_t_ref):
        attn = source[...].reshape(ZN * HD, 256)
        chosen = lax.dot_general(pick, attn, (((1,), (1,)), ((), ())), preferred_element_type=f32)
        picked.append(chosen.astype(bf16))

    def product(weight, low, high):
        return sum(jnp.dot(picked[t][:, low:high], weight[t], preferred_element_type=f32) for t in range(2))

    blocks[me] = product(own, 0, 640)
    blocks[lax.rem(me + 1, SECTIONS)] = product(right, 0, 640)
    blocks[lax.rem(me + 3, SECTIONS)] = product(left, 0, 640)
    blocks[lax.rem(me + 2, SECTIONS)] = product(opp_a, 0, 320) + product(opp_b, 320, 640)
    total = jnp.dot(pick, patch_ref[...], preferred_element_type=f32)
    total += jnp.concatenate([blocks[section] for section in range(SECTIONS)], axis=1)
    out_ref[...] = rms_norm(total, gain_ref[...]).astype(bf16)


def merger_kernel(sizes, place_ref, *refs):
    count = len(sizes)
    sources, (up_ref, down_ref), outs, tokens = refs[:count], refs[count : count + 2], refs[count + 2 : -1], refs[-1]
    tp = place_ref[3]
    place = 0
    for source, size in zip(sources, sizes):
        for part in range(size // 128):
            half = jnp.bitwise_xor(tp, place % 2)
            rows = pl.ds(pl.multiple_of(place // 2 * 64 + half * 32, 32), 32)
            for j in range(4):
                low = part * 128 + j * 32
                tokens[j, rows, :] = source[low : low + 32, :]
            place += 1
    hidden = jnp.zeros((place * 32, 320), f32)
    for j in range(4):
        hidden += jnp.dot(tokens[j], up_ref[j * 1280 : (j + 1) * 1280, :], preferred_element_type=f32)
    hidden = (0.5 * hidden * (1.0 + lax.erf(hidden * (0.5**0.5)))).astype(bf16)
    for k in range(7):
        columns = slice(k * 512, (k + 1) * 512)
        made = jnp.dot(hidden, down_ref[:, columns], preferred_element_type=f32).astype(bf16)
        for n, out in enumerate(outs):
            out[:, columns] = made[n * 32 : (n + 1) * 32]


def merge(place, pieces, merger_up, merger_down, name):
    sizes = [piece.shape[0] for piece in pieces]
    total = sum(sizes) // 4
    return call(
        functools.partial(merger_kernel, sizes),
        tuple(jax.ShapeDtypeStruct((32, 3584), bf16) for _ in range(total // 32)),
        [SMEM] + [VMEM] * (len(pieces) + 2),
        [pltpu.VMEM((4, total, 1280), bf16)],
        flops=2 * 256 * 320 * (5120 + 3584),
        moved=6000000,
        name=name,
    )(place, *pieces, merger_up, merger_down)


def send(value, distance, flip):
    route = [(s * 2 + t, (s + distance) % SECTIONS * 2 + (t ^ flip)) for s in range(SECTIONS) for t in range(2)]
    return lax.ppermute(value, ("section", "tp"), route)


def on_device(patches, frame_ids, groups, norm_gain, qkv_weight, out_weight, merge_gain, merger_up, merger_down):
    me, blk, tp = lax.axis_index("section"), lax.axis_index("blk"), lax.axis_index("tp")
    core, y = blk % 2, blk // 16
    place = jnp.stack([me, core, y, tp]).astype(jnp.int32)
    patch = patches[0]
    normed = rms_norm(patch.astype(f32), norm_gain).astype(bf16)

    kv_own, q_own = qkv_weight[1:3], qkv_weight[0:1]
    out_half = tp_swap(lax.dynamic_slice_in_dim(out_weight, core * 160, 160, axis=1))
    kv_mine, out_half = fetch(kv_own, core, out_half)
    kv_mine, q_own = lax.optimization_barrier((kv_mine, q_own))
    kv = z_exchange(project(place, normed, kv_own, kv_mine, 1.0))
    out_rest = blk_swap(out_half, 1)
    out_weight_t = jnp.where(
        core == 0, jnp.concatenate([out_half, out_rest], axis=1), jnp.concatenate([out_rest, out_half], axis=1)
    )
    q_mine, out_own = lax.optimization_barrier((fetch(q_own, core)[0], jnp.stack([out_weight, out_weight_t])))
    out_right, out_left = section_shift(out_own, -1), section_shift(out_own, 1)
    q = project(place, normed, q_own, q_mine, HD ** (-0.5) * math.log2(math.e))
    kv, q = lax.optimization_barrier((kv, q))
    far = blk_swap(kv, 16)
    near = blk_swap(kv, 1)
    q = z_exchange(q)
    far, q, out_right, out_left = lax.optimization_barrier((far, q, out_right, out_left))
    across = blk_swap(far, 1)
    out_a, out_b = section_shift(out_right[:, :320], -1), section_shift(out_left[:, 320:], 1)

    attn = z_exchange(attention(place, frame_ids[0], q, (kv, near, far, across), y, core))
    attn_t = tp_swap(attn)
    order = groups[0].reshape(2, 32, 4).transpose(0, 2, 1).reshape(256, 1)
    own = call(
        output_kernel,
        jax.ShapeDtypeStruct((256, 1280), bf16),
        [SMEM] + [VMEM] * 10,
        [pltpu.VMEM((SECTIONS, 256, 320), f32)],
        flops=2 * 256 * 1280 * 1800,
        moved=5000000,
        name="output",
    )(place, order, merge_gain[None, :], patch, attn, attn_t, out_own, out_right, out_left, out_a, out_b)

    right, left = section_shift(own, -1), section_shift(own, 1)
    own_same, own_other = merge(place, [own], merger_up, merger_down, "merge_own")
    right, left, own_same, own_other = lax.optimization_barrier((right, left, own_same, own_other))
    opp_a, opp_b = section_shift(right[:128], -1), section_shift(left[128:], 1)
    sums = [send(own_same, 1, 0), send(own_other, 1, 1)]
    right_same, right_other, left_same, left_other = merge(
        place, [right, left], merger_up, merger_down, "merge_next"
    )
    sums += [send(right_same, 2, 0), send(right_other, 2, 1), left_same, send(left_other, 0, 1)]
    opp_same, opp_other = merge(place, [opp_a, opp_b], merger_up, merger_down, "merge_opposite")
    sums += [send(opp_same, 3, 0), send(opp_other, 3, 1)]
    return sum(part.astype(f32) for part in sums).astype(bf16)[None]


def solution(mesh):
    in_specs = (
        P("section", "blk", None),
        P("section", None),
        P("section", "blk", None),
        P(),
        P(None, "section", "tp"),
        P("tp", "section"),
        P(),
        P(None, ("section", "tp")),
        P(("section", "tp"), None),
    )
    out_specs = P("section", ("blk", "tp"), None)
    return jax.shard_map(on_device, mesh=mesh, in_specs=in_specs, out_specs=out_specs, check_vma=False)
```

```python
import functools
import math

import jax
import jax.numpy as jnp
from jax import lax
from jax.experimental import pallas as pl
from jax.experimental.pallas import tpu as pltpu
from jax.sharding import PartitionSpec as P

HD = 80
ZN = 8
KB = 512
FAR, NEAR = (0, 3, 4, 5), (1, 2, 6, 7)
SECTIONS = 4
VMEM = pl.BlockSpec(memory_space=pltpu.VMEM)
SMEM = pl.BlockSpec(memory_space=pltpu.SMEM)
MIB = 1024 * 1024
bf16, f32 = jnp.bfloat16, jnp.float32

Z_GROUPS = [[y * 16 + z * 2 + c for z in range(ZN)] for y in range(2) for c in range(2)]


def call(kernel, out_shape, specs, scratch=(), flops=0, moved=0, name=None, grant=14):
    return pl.pallas_call(
        kernel,
        out_shape=out_shape,
        in_specs=specs,
        out_specs=jax.tree.map(lambda _: VMEM, out_shape),
        scratch_shapes=list(scratch),
        compiler_params=pltpu.CompilerParams(vmem_limit_bytes=grant * MIB),
        cost_estimate=pl.CostEstimate(flops=flops, bytes_accessed=moved, transcendentals=0),
        name=name,
    )


def section_shift(value, distance):
    route = [(i, (i + distance) % SECTIONS) for i in range(SECTIONS)]
    return lax.ppermute(value, "section", route)


def blk_swap(value, bit):
    return lax.ppermute(value, "blk", [(i, i ^ bit) for i in range(32)])


def tp_swap(value):
    return lax.ppermute(value, "tp", [(0, 1), (1, 0)])


def z_exchange(value):
    return lax.all_to_all(value, "blk", 0, 0, axis_index_groups=Z_GROUPS, tiled=True)


def rms_norm(value, gain):
    return value * lax.rsqrt(jnp.mean(value * value, axis=-1, keepdims=True) + 1e-06) * gain


def project_kernel(scale, count, place_ref, normed_ref, own_ref, mine_ref, other_ref, out_ref, weight):
    me, core = place_ref[0], place_ref[1]
    row = lambda section, half: pl.ds(pl.multiple_of(section * 320 + half * 160, 16), 160)
    for t in range(count):
        weight[t, pl.ds(pl.multiple_of(me * 320, 16), 320), :] = own_ref[t]
        for source, half in ((mine_ref, core), (other_ref, 1 - core)):
            for k in range(3):
                section = lax.rem(me + k + 1, SECTIONS)
                weight[t, row(section, half), :] = source[k, t]
        made = jnp.dot(normed_ref[...], weight[t], preferred_element_type=f32)
        turned = (made * scale).T.astype(bf16)
        for h in range(ZN):
            out_ref[h, t * HD : (t + 1) * HD, :] = turned[h * HD : (h + 1) * HD, :]


def fetch(own, core, *beside):
    half = lax.dynamic_slice_in_dim(own, core * 160, 160, axis=1)
    right, left, *beside = lax.optimization_barrier((section_shift(half, -1), section_shift(half, 1), *beside))
    opp_a, opp_b = section_shift(right[:, :80], -1), section_shift(left[:, 80:], 1)
    return jnp.stack([right, jnp.concatenate([opp_a, opp_b], axis=1), left]), *beside


def project(place, normed, own, mine, scale):
    count = own.shape[0]
    other = blk_swap(mine, 1)
    return call(
        functools.partial(project_kernel, scale, count),
        jax.ShapeDtypeStruct((ZN, count * HD, 256), bf16),
        [SMEM] + [VMEM] * 4,
        [pltpu.VMEM((count, 1280, 640), bf16)],
        flops=2 * 256 * 1280 * 640 * count,
        moved=count * 2 * 1280 * 640,
        name="project",
    )(place, normed, own, mine, other)


def attention_kernel(bounds_ref, place_ref, qframe_ref, kframe_ref, q_ref, own, near, far, across, out_ref, keys, values, held):
    y, core = place_ref[2], place_ref[1]
    filler = (lax.broadcasted_iota(jnp.int32, (48, 256), 0) == 0).astype(f32).astype(bf16)
    frame = lax.broadcasted_iota(jnp.int32, (16, 256), 0)

    def arrange(z, unused):
        for which, source in enumerate((own, near, far, across)):
            y_of = jnp.bitwise_xor(y, which // 2)
            core_of = jnp.bitwise_xor(core, which % 2)
            place = pl.ds(pl.multiple_of((y_of * 16 + z * 2 + core_of) * 256, 256), 256)
            keys[:HD, place] = source[z, :HD, :]
            other = (frame < 4) & (frame != kframe_ref[:, place])
            keys[HD:, place] = jnp.where(other, -1e30, 0.0).astype(bf16)
            values[place, :] = jnp.concatenate([source[z, HD:, :], filler], axis=0).T
        return unused

    lax.fori_loop(0, ZN, arrange, 0)

    def one_block(n, unused):
        block = bounds_ref[2, n]
        tag = (frame == qframe_ref[pl.ds(block, 1), :]).astype(f32).astype(bf16)
        query = jnp.concatenate([q_ref[block], tag], axis=0).T
        first, last = bounds_ref[0, n], bounds_ref[1, n]

        def part(index):
            return pl.ds(pl.multiple_of(index * KB, KB), KB)

        def scores_of(index):
            return jnp.dot(query, keys[:, part(index)], preferred_element_type=f32)

        def absorb(scores, index, carry):
            top, accum = carry
            new_top = jnp.maximum(top, jnp.max(scores, axis=1, keepdims=True))
            weights = jnp.exp2(scores - new_top).astype(bf16)
            product = jnp.dot(weights, values[part(index), :], preferred_element_type=f32)
            return new_top, accum * jnp.exp2(top - new_top) + product

        def run(length, start, count, carry):
            def body(step, carry):
                index = start + length * step
                for k in range(length):
                    scores = held[k % 2]
                    held[(k + 1) % 2] = scores_of(jnp.minimum(index + k + 1, last - 1))
                    carry = absorb(scores, index + k, carry)
                return carry

            return lax.fori_loop(0, count, body, carry)

        held[0] = scores_of(first)
        carry = (jnp.full((256, 1), -1e30, f32), jnp.zeros((256, 128), f32))
        fours = (last - first) // 4
        carry = run(4, first, fours, carry)
        rest = first + 4 * fours
        twos = (last - rest) // 2
        carry = run(2, rest, twos, carry)
        carry = lax.fori_loop(rest + 2 * twos, last, lambda index, c: absorb(held[0], index, c), carry)
        accum = carry[1]
        result = accum / accum[:, HD : HD + 1]
        out_ref[n] = result.T[:HD, :].astype(bf16)
        return unused

    lax.fori_loop(0, 4, one_block, 0)


def attention(place, frames, q, sources, y, z, core, shifts):
    ends = jnp.sum((frames[None, :] <= jnp.arange(-1, 4)[:, None]).astype(jnp.int32), axis=1)
    grid = frames.reshape(2, ZN, 2, 256)
    mine = lax.dynamic_index_in_dim(lax.dynamic_index_in_dim(grid, y, 0, False), core, 1, False)
    start, stop = ends[mine[:, 0]], ends[mine[:, -1] + 1]
    blocks = (z + jnp.array(shifts)) % ZN
    bounds = jnp.stack([(start // KB)[blocks], ((stop + KB - 1) // KB)[blocks], blocks]).astype(jnp.int32)
    return call(
        attention_kernel,
        jax.ShapeDtypeStruct((4, HD, 256), bf16),
        [SMEM, SMEM] + [VMEM] * 7,
        [pltpu.VMEM((HD + 16, 8192), bf16), pltpu.VMEM((8192, 128), bf16), pltpu.VMEM((2, 256, KB), f32)],
        flops=4 * 2048 * 4096 * 256,
        moved=4 * 8192 * HD,
        name="attention",
    )(bounds, place, mine, frames[None, :], q, *sources)


def z_shift(value, distance):
    return lax.ppermute(value, "blk", [(i, i // 16 * 16 + (i + 2 * distance) % 16) for i in range(32)])


def output_kernel(
    place_ref, order_ref, gain_ref, patch_ref, far, near, far_t, near_t, own, right, left, opp_a, opp_b, out_ref, attn, blocks
):
    me = place_ref[0]
    pick = (order_ref[...] == lax.broadcasted_iota(jnp.int32, (256, 256), 1)).astype(f32).astype(bf16)
    for t, (away, close) in enumerate(((far, near), (far_t, near_t))):
        for source, shifts in ((away, FAR), (close, NEAR)):
            for n, shift in enumerate(shifts):
                head = lax.rem(place_ref[4] + ZN - shift, ZN)
                attn[t, pl.ds(pl.multiple_of(head * HD, 16), HD), :] = source[n]
    picked = []
    for t in range(2):
        chosen = lax.dot_general(pick, attn[t], (((1,), (1,)), ((), ())), preferred_element_type=f32)
        picked.append(chosen.astype(bf16))

    def product(weight, low, high):
        return sum(jnp.dot(picked[t][:, low:high], weight[t], preferred_element_type=f32) for t in range(2))

    blocks[me] = product(own, 0, 640)
    blocks[lax.rem(me + 1, SECTIONS)] = product(right, 0, 640)
    blocks[lax.rem(me + 3, SECTIONS)] = product(left, 0, 640)
    blocks[lax.rem(me + 2, SECTIONS)] = product(opp_a, 0, 320) + product(opp_b, 320, 640)
    total = jnp.dot(pick, patch_ref[...], preferred_element_type=f32)
    total += jnp.concatenate([blocks[section] for section in range(SECTIONS)], axis=1)
    out_ref[...] = rms_norm(total, gain_ref[...]).astype(bf16)


def merger_kernel(sizes, place_ref, *refs):
    count = len(sizes)
    sources, (up_ref, down_ref), outs, tokens = refs[:count], refs[count : count + 2], refs[count + 2 : -1], refs[-1]
    tp = place_ref[3]
    place = 0
    for source, size in zip(sources, sizes):
        for part in range(size // 128):
            half = jnp.bitwise_xor(tp, place % 2)
            rows = pl.ds(pl.multiple_of(place // 2 * 64 + half * 32, 32), 32)
            for j in range(4):
                low = part * 128 + j * 32
                tokens[j, rows, :] = source[low : low + 32, :]
            place += 1
    hidden = jnp.zeros((place * 32, 320), f32)
    for j in range(4):
        hidden += jnp.dot(tokens[j], up_ref[j * 1280 : (j + 1) * 1280, :], preferred_element_type=f32)
    hidden = (0.5 * hidden * (1.0 + lax.erf(hidden * (0.5**0.5)))).astype(bf16)
    for k in range(7):
        columns = slice(k * 512, (k + 1) * 512)
        made = jnp.dot(hidden, down_ref[:, columns], preferred_element_type=f32).astype(bf16)
        for n, out in enumerate(outs):
            out[:, columns] = made[n * 32 : (n + 1) * 32]


def merge(place, pieces, merger_up, merger_down, name):
    sizes = [piece.shape[0] for piece in pieces]
    total = sum(sizes) // 4
    return call(
        functools.partial(merger_kernel, sizes),
        tuple(jax.ShapeDtypeStruct((32, 3584), bf16) for _ in range(total // 32)),
        [SMEM] + [VMEM] * (len(pieces) + 2),
        [pltpu.VMEM((4, total, 1280), bf16)],
        flops=2 * 256 * 320 * (5120 + 3584),
        moved=6000000,
        name=name,
    )(place, *pieces, merger_up, merger_down)


def send(value, distance, flip):
    route = [(s * 2 + t, (s + distance) % SECTIONS * 2 + (t ^ flip)) for s in range(SECTIONS) for t in range(2)]
    return lax.ppermute(value, ("section", "tp"), route)


def on_device(patches, frame_ids, groups, norm_gain, qkv_weight, out_weight, merge_gain, merger_up, merger_down):
    me, blk, tp = lax.axis_index("section"), lax.axis_index("blk"), lax.axis_index("tp")
    core, y, z = blk % 2, blk // 16, blk // 2 % ZN
    place = jnp.stack([me, core, y, tp, z]).astype(jnp.int32)
    patch = patches[0]
    normed = rms_norm(patch.astype(f32), norm_gain).astype(bf16)

    kv_own, q_own = qkv_weight[1:3], qkv_weight[0:1]
    out_half = tp_swap(lax.dynamic_slice_in_dim(out_weight, core * 160, 160, axis=1))
    kv_mine, out_half = fetch(kv_own, core, out_half)
    kv_mine, q_own = lax.optimization_barrier((kv_mine, q_own))
    kv = z_exchange(project(place, normed, kv_own, kv_mine, 1.0))
    out_rest = blk_swap(out_half, 1)
    out_weight_t = jnp.where(
        core == 0, jnp.concatenate([out_half, out_rest], axis=1), jnp.concatenate([out_rest, out_half], axis=1)
    )
    q_mine, out_own = lax.optimization_barrier((fetch(q_own, core)[0], jnp.stack([out_weight, out_weight_t])))
    out_right, out_left = section_shift(out_own, -1), section_shift(out_own, 1)
    q = project(place, normed, q_own, q_mine, HD ** (-0.5) * math.log2(math.e))
    kv, q = lax.optimization_barrier((kv, q))
    far = blk_swap(kv, 16)
    near = blk_swap(kv, 1)
    q = z_exchange(q)
    far, q, out_right, out_left = lax.optimization_barrier((far, q, out_right, out_left))
    across = blk_swap(far, 1)
    out_a, out_b = section_shift(out_right[:, :320], -1), section_shift(out_left[:, 320:], 1)

    sources = (kv, near, far, across)
    first = attention(place, frame_ids[0], q, sources, y, z, core, FAR)
    moved = [z_shift(first[n], FAR[n]) for n in range(1, 4)]
    second = attention(place, frame_ids[0], q, sources, y, z, core, NEAR)
    second, out_a, out_b, *moved = lax.optimization_barrier((second, out_a, out_b, *moved))
    far_heads = jnp.stack([first[0], *moved])
    near_heads = jnp.stack([z_shift(second[n], NEAR[n]) for n in range(4)])
    far_heads_t, near_heads_t = tp_swap(far_heads), tp_swap(near_heads)
    order = groups[0].reshape(2, 32, 4).transpose(0, 2, 1).reshape(256, 1)
    own = call(
        output_kernel,
        jax.ShapeDtypeStruct((256, 1280), bf16),
        [SMEM] + [VMEM] * 12,
        [pltpu.VMEM((2, ZN * HD, 256), bf16), pltpu.VMEM((SECTIONS, 256, 320), f32)],
        flops=2 * 256 * 1280 * 1800,
        moved=5000000,
        name="output",
    )(place, order, merge_gain[None, :], patch, far_heads, near_heads, far_heads_t, near_heads_t, out_own, out_right, out_left, out_a, out_b)

    right, left = section_shift(own, -1), section_shift(own, 1)
    own_same, own_other = merge(place, [own], merger_up, merger_down, "merge_own")
    right, left, own_same, own_other = lax.optimization_barrier((right, left, own_same, own_other))
    opp_a, opp_b = section_shift(right[:128], -1), section_shift(left[128:], 1)
    sums = [send(own_same, 1, 0), send(own_other, 1, 1)]
    right_same, right_other, left_same, left_other = merge(
        place, [right, left], merger_up, merger_down, "merge_next"
    )
    sums += [send(right_same, 2, 0), send(right_other, 2, 1), left_same, send(left_other, 0, 1)]
    opp_same, opp_other = merge(place, [opp_a, opp_b], merger_up, merger_down, "merge_opposite")
    sums += [send(opp_same, 3, 0), send(opp_other, 3, 1)]
    return sum(part.astype(f32) for part in sums).astype(bf16)[None]


def solution(mesh):
    in_specs = (
        P("section", "blk", None),
        P("section", None),
        P("section", "blk", None),
        P(),
        P(None, "section", "tp"),
        P("tp", "section"),
        P(),
        P(None, ("section", "tp")),
        P(("section", "tp"), None),
    )
    out_specs = P("section", ("blk", "tp"), None)
    return jax.shard_map(on_device, mesh=mesh, in_specs=in_specs, out_specs=out_specs, check_vma=False)
```

```python
import functools
import math

import jax
import jax.numpy as jnp
from jax import lax
from jax.experimental import pallas as pl
from jax.experimental.pallas import tpu as pltpu
from jax.sharding import PartitionSpec as P

HD = 80
ZN = 8
KB = 512
SECTIONS = 4
VMEM = pl.BlockSpec(memory_space=pltpu.VMEM)
SMEM = pl.BlockSpec(memory_space=pltpu.SMEM)
MIB = 1024 * 1024
bf16, f32 = jnp.bfloat16, jnp.float32

Z_GROUPS = [[y * 16 + z * 2 + c for z in range(ZN)] for y in range(2) for c in range(2)]


def call(kernel, out_shape, specs, scratch=(), flops=0, moved=0, name=None, grant=14):
    return pl.pallas_call(
        kernel,
        out_shape=out_shape,
        in_specs=specs,
        out_specs=jax.tree.map(lambda _: VMEM, out_shape),
        scratch_shapes=list(scratch),
        compiler_params=pltpu.CompilerParams(vmem_limit_bytes=grant * MIB),
        cost_estimate=pl.CostEstimate(flops=flops, bytes_accessed=moved, transcendentals=0),
        name=name,
    )


def section_shift(value, distance):
    route = [(i, (i + distance) % SECTIONS) for i in range(SECTIONS)]
    return lax.ppermute(value, "section", route)


def blk_swap(value, bit):
    return lax.ppermute(value, "blk", [(i, i ^ bit) for i in range(32)])


def tp_swap(value):
    return lax.ppermute(value, "tp", [(0, 1), (1, 0)])


def z_exchange(value):
    return lax.all_to_all(value, "blk", 0, 0, axis_index_groups=Z_GROUPS, tiled=True)


def rms_norm(value, gain):
    return value * lax.rsqrt(jnp.mean(value * value, axis=-1, keepdims=True) + 1e-06) * gain


def project_kernel(scale, low, count, place_ref, normed_ref, own_ref, mine_ref, other_ref, out_ref, weight):
    me, core = place_ref[0], place_ref[1]
    row = lambda section, half: pl.ds(pl.multiple_of(section * 320 + half * 160, 16), 160)
    for t in range(count):
        weight[t, pl.ds(pl.multiple_of(me * 320, 16), 320), :] = own_ref[low + t]
        for source, half in ((mine_ref, core), (other_ref, 1 - core)):
            for k in range(3):
                section = lax.rem(me + k + 1, SECTIONS)
                weight[t, row(section, half), :] = source[k, t]
        made = jnp.dot(normed_ref[...], weight[t], preferred_element_type=f32)
        turned = (made * scale).T.astype(bf16)
        for h in range(ZN):
            out_ref[h, t * HD : (t + 1) * HD, :] = turned[h * HD : (h + 1) * HD, :]


def fetch(weight, low, count, core, *beside):
    half = lax.dynamic_slice(weight, (low, core * 160, 0), (count, 160, weight.shape[2]))
    right, left, *beside = lax.optimization_barrier((section_shift(half, -1), section_shift(half, 1), *beside))
    opp_a, opp_b = section_shift(right[:, :80], -1), section_shift(left[:, 80:], 1)
    return jnp.stack([right, jnp.concatenate([opp_a, opp_b], axis=1), left]), *beside


def project(place, normed, weight, low, mine, scale):
    count = mine.shape[1]
    other = blk_swap(mine, 1)
    return call(
        functools.partial(project_kernel, scale, low, count),
        jax.ShapeDtypeStruct((ZN, count * HD, 256), bf16),
        [SMEM] + [VMEM] * 4,
        [pltpu.VMEM((count, 1280, 640), bf16)],
        flops=2 * 256 * 1280 * 640 * count,
        moved=count * 2 * 1280 * 640,
        name="project",
    )(place, normed, weight, mine, other)


def attention_kernel(bounds_ref, place_ref, qframe_ref, kframe_ref, q_ref, own, near, far, across, out_ref, keys, values, held):
    y, core = place_ref[2], place_ref[1]
    filler = (lax.broadcasted_iota(jnp.int32, (48, 256), 0) == 0).astype(f32).astype(bf16)
    frame = lax.broadcasted_iota(jnp.int32, (16, 256), 0)

    def arrange(z, unused):
        for which, source in enumerate((own, near, far, across)):
            y_of = jnp.bitwise_xor(y, which // 2)
            core_of = jnp.bitwise_xor(core, which % 2)
            place = pl.ds(pl.multiple_of((y_of * 16 + z * 2 + core_of) * 256, 256), 256)
            keys[:HD, place] = source[z, :HD, :]
            other = (frame < 4) & (frame != kframe_ref[:, place])
            keys[HD:, place] = jnp.where(other, -1e30, 0.0).astype(bf16)
            values[place, :] = jnp.concatenate([source[z, HD:, :], filler], axis=0).T
        return unused

    lax.fori_loop(0, ZN, arrange, 0)

    def one_block(block, unused):
        tag = (frame == qframe_ref[pl.ds(block, 1), :]).astype(f32).astype(bf16)
        query = jnp.concatenate([q_ref[block], tag], axis=0).T
        first, last = bounds_ref[0, block], bounds_ref[1, block]

        def part(index):
            return pl.ds(pl.multiple_of(index * KB, KB), KB)

        def scores_of(index):
            return jnp.dot(query, keys[:, part(index)], preferred_element_type=f32)

        def absorb(scores, index, carry):
            top, accum = carry
            new_top = jnp.maximum(top, jnp.max(scores, axis=1, keepdims=True))
            weights = jnp.exp2(scores - new_top).astype(bf16)
            product = jnp.dot(weights, values[part(index), :], preferred_element_type=f32)
            return new_top, accum * jnp.exp2(top - new_top) + product

        def run(length, start, count, carry):
            def body(step, carry):
                index = start + length * step
                for k in range(length):
                    scores = held[k % 2]
                    held[(k + 1) % 2] = scores_of(jnp.minimum(index + k + 1, last - 1))
                    carry = absorb(scores, index + k, carry)
                return carry

            return lax.fori_loop(0, count, body, carry)

        held[0] = scores_of(first)
        carry = (jnp.full((256, 1), -1e30, f32), jnp.zeros((256, 128), f32))
        fours = (last - first) // 4
        carry = run(4, first, fours, carry)
        rest = first + 4 * fours
        twos = (last - rest) // 2
        carry = run(2, rest, twos, carry)
        carry = lax.fori_loop(rest + 2 * twos, last, lambda index, c: absorb(held[0], index, c), carry)
        accum = carry[1]
        result = accum / accum[:, HD : HD + 1]
        out_ref[block] = result.T[:HD, :].astype(bf16)
        return unused

    lax.fori_loop(0, ZN, one_block, 0)


def attention(place, frames, q, sources, y, core):
    ends = jnp.sum((frames[None, :] <= jnp.arange(-1, 4)[:, None]).astype(jnp.int32), axis=1)
    grid = frames.reshape(2, ZN, 2, 256)
    mine = lax.dynamic_index_in_dim(lax.dynamic_index_in_dim(grid, y, 0, False), core, 1, False)
    start, stop = ends[mine[:, 0]], ends[mine[:, -1] + 1]
    bounds = jnp.stack([start // KB, (stop + KB - 1) // KB]).astype(jnp.int32)
    return call(
        attention_kernel,
        jax.ShapeDtypeStruct((ZN, HD, 256), bf16),
        [SMEM, SMEM] + [VMEM] * 7,
        [pltpu.VMEM((HD + 16, 8192), bf16), pltpu.VMEM((8192, 128), bf16), pltpu.VMEM((2, 256, KB), f32)],
        flops=4 * 2048 * 4096 * 256,
        moved=4 * 8192 * HD,
        name="attention",
    )(bounds, place, mine, frames[None, :], q, *sources)


def output_kernel(
    place_ref, order_ref, gain_ref, patch_ref, attn_ref, attn_t_ref, own, right, left, opp_a, opp_b, out_ref, blocks
):
    me = place_ref[0]
    pick = (order_ref[...] == lax.broadcasted_iota(jnp.int32, (256, 256), 1)).astype(f32).astype(bf16)
    picked = []
    for source in (attn_ref, attn_t_ref):
        attn = source[...].reshape(ZN * HD, 256)
        chosen = lax.dot_general(pick, attn, (((1,), (1,)), ((), ())), preferred_element_type=f32)
        picked.append(chosen.astype(bf16))

    def product(weight, low, high):
        return sum(jnp.dot(picked[t][:, low:high], weight[t], preferred_element_type=f32) for t in range(2))

    blocks[me] = product(own, 0, 640)
    blocks[lax.rem(me + 1, SECTIONS)] = product(right, 0, 640)
    blocks[lax.rem(me + 3, SECTIONS)] = product(left, 0, 640)
    blocks[lax.rem(me + 2, SECTIONS)] = product(opp_a, 0, 320) + product(opp_b, 320, 640)
    total = jnp.dot(pick, patch_ref[...], preferred_element_type=f32)
    total += jnp.concatenate([blocks[section] for section in range(SECTIONS)], axis=1)
    out_ref[...] = rms_norm(total, gain_ref[...]).astype(bf16)


def merger_kernel(sizes, place_ref, *refs):
    count = len(sizes)
    sources, (up_ref, down_ref), outs, tokens = refs[:count], refs[count : count + 2], refs[count + 2 : -1], refs[-1]
    tp = place_ref[3]
    place = 0
    for source, size in zip(sources, sizes):
        for part in range(size // 128):
            half = jnp.bitwise_xor(tp, place % 2)
            rows = pl.ds(pl.multiple_of(place // 2 * 64 + half * 32, 32), 32)
            for j in range(4):
                low = part * 128 + j * 32
                tokens[j, rows, :] = source[low : low + 32, :]
            place += 1
    hidden = jnp.zeros((place * 32, 320), f32)
    for j in range(4):
        hidden += jnp.dot(tokens[j], up_ref[j * 1280 : (j + 1) * 1280, :], preferred_element_type=f32)
    hidden = (0.5 * hidden * (1.0 + lax.erf(hidden * (0.5**0.5)))).astype(bf16)
    for k in range(7):
        columns = slice(k * 512, (k + 1) * 512)
        made = jnp.dot(hidden, down_ref[:, columns], preferred_element_type=f32).astype(bf16)
        for n, out in enumerate(outs):
            out[:, columns] = made[n * 32 : (n + 1) * 32]


def merge(place, pieces, merger_up, merger_down, name):
    sizes = [piece.shape[0] for piece in pieces]
    total = sum(sizes) // 4
    return call(
        functools.partial(merger_kernel, sizes),
        tuple(jax.ShapeDtypeStruct((32, 3584), bf16) for _ in range(total // 32)),
        [SMEM] + [VMEM] * (len(pieces) + 2),
        [pltpu.VMEM((4, total, 1280), bf16)],
        flops=2 * 256 * 320 * (5120 + 3584),
        moved=6000000,
        name=name,
    )(place, *pieces, merger_up, merger_down)


def send(value, distance, flip):
    route = [(s * 2 + t, (s + distance) % SECTIONS * 2 + (t ^ flip)) for s in range(SECTIONS) for t in range(2)]
    return lax.ppermute(value, ("section", "tp"), route)


def on_device(patches, frame_ids, groups, norm_gain, qkv_weight, out_weight, merge_gain, merger_up, merger_down):
    me, blk, tp = lax.axis_index("section"), lax.axis_index("blk"), lax.axis_index("tp")
    core, y = blk % 2, blk // 16
    place = jnp.stack([me, core, y, tp]).astype(jnp.int32)
    patch = patches[0]
    normed = rms_norm(patch.astype(f32), norm_gain).astype(bf16)

    out_half = tp_swap(lax.dynamic_slice_in_dim(out_weight, core * 160, 160, axis=1))
    kv_mine, out_half = fetch(qkv_weight, 1, 2, core, out_half)
    kv_mine, later = lax.optimization_barrier((kv_mine, qkv_weight))
    kv = z_exchange(project(place, normed, qkv_weight, 1, kv_mine, 1.0))
    (q_mine,) = fetch(later, 0, 1, core)
    q = project(place, normed, qkv_weight, 0, q_mine, HD ** (-0.5) * math.log2(math.e))
    kv, q, out_half = lax.optimization_barrier((kv, q, out_half))
    far = blk_swap(kv, 16)
    near = blk_swap(kv, 1)
    q = z_exchange(q)
    out_rest = blk_swap(out_half, 1)
    out_weight_t = jnp.where(
        core == 0, jnp.concatenate([out_half, out_rest], axis=1), jnp.concatenate([out_rest, out_half], axis=1)
    )
    far, q, out_own = lax.optimization_barrier((far, q, jnp.stack([out_weight, out_weight_t])))
    across = blk_swap(far, 1)

    out_right, out_left = section_shift(out_own, -1), section_shift(out_own, 1)
    attn = attention(place, frame_ids[0], q, (kv, near, far, across), y, core)
    attn, out_right, out_left = lax.optimization_barrier((attn, out_right, out_left))
    attn = z_exchange(attn)
    out_a, out_b = section_shift(out_right[:, :320], -1), section_shift(out_left[:, 320:], 1)
    attn_t = tp_swap(attn)
    order = groups[0].reshape(2, 32, 4).transpose(0, 2, 1).reshape(256, 1)
    own = call(
        output_kernel,
        jax.ShapeDtypeStruct((256, 1280), bf16),
        [SMEM] + [VMEM] * 10,
        [pltpu.VMEM((SECTIONS, 256, 320), f32)],
        flops=2 * 256 * 1280 * 1800,
        moved=5000000,
        name="output",
    )(place, order, merge_gain[None, :], patch, attn, attn_t, out_own, out_right, out_left, out_a, out_b)

    right, left = section_shift(own, -1), section_shift(own, 1)
    own_same, own_other = merge(place, [own], merger_up, merger_down, "merge_own")
    right, left, own_same, own_other = lax.optimization_barrier((right, left, own_same, own_other))
    opp_a, opp_b = section_shift(right[:128], -1), section_shift(left[128:], 1)
    sums = [send(own_same, 1, 0), send(own_other, 1, 1)]
    right_same, right_other, left_same, left_other = merge(
        place, [right, left], merger_up, merger_down, "merge_next"
    )
    sums += [send(right_same, 2, 0), send(right_other, 2, 1), left_same, send(left_other, 0, 1)]
    opp_same, opp_other = merge(place, [opp_a, opp_b], merger_up, merger_down, "merge_opposite")
    sums += [send(opp_same, 3, 0), send(opp_other, 3, 1)]
    return sum(part.astype(f32) for part in sums).astype(bf16)[None]


def solution(mesh):
    in_specs = (
        P("section", "blk", None),
        P("section", None),
        P("section", "blk", None),
        P(),
        P(None, "section", "tp"),
        P("tp", "section"),
        P(),
        P(None, ("section", "tp")),
        P(("section", "tp"), None),
    )
    out_specs = P("section", ("blk", "tp"), None)
    return jax.shard_map(on_device, mesh=mesh, in_specs=in_specs, out_specs=out_specs, check_vma=False)
```

```python
import functools
import math

import jax
import jax.numpy as jnp
from jax import lax
from jax.experimental import pallas as pl
from jax.experimental.pallas import tpu as pltpu
from jax.sharding import PartitionSpec as P

HD = 80
ZN = 8
KB = 512
SECTIONS = 4
VMEM = pl.BlockSpec(memory_space=pltpu.VMEM)
SMEM = pl.BlockSpec(memory_space=pltpu.SMEM)
MIB = 1024 * 1024
bf16, f32 = jnp.bfloat16, jnp.float32

Z_GROUPS = [[y * 16 + z * 2 + c for z in range(ZN)] for y in range(2) for c in range(2)]


def call(kernel, out_shape, specs, scratch=(), flops=0, moved=0, name=None, grant=14):
    return pl.pallas_call(
        kernel,
        out_shape=out_shape,
        in_specs=specs,
        out_specs=jax.tree.map(lambda _: VMEM, out_shape),
        scratch_shapes=list(scratch),
        compiler_params=pltpu.CompilerParams(vmem_limit_bytes=grant * MIB),
        cost_estimate=pl.CostEstimate(flops=flops, bytes_accessed=moved, transcendentals=0),
        name=name,
    )


def section_shift(value, distance):
    route = [(i, (i + distance) % SECTIONS) for i in range(SECTIONS)]
    return lax.ppermute(value, "section", route)


def blk_swap(value, bit):
    return lax.ppermute(value, "blk", [(i, i ^ bit) for i in range(32)])


def tp_swap(value):
    return lax.ppermute(value, "tp", [(0, 1), (1, 0)])


def z_exchange(value):
    return lax.all_to_all(value, "blk", 0, 0, axis_index_groups=Z_GROUPS, tiled=True)


def rms_norm(value, gain):
    return value * lax.rsqrt(jnp.mean(value * value, axis=-1, keepdims=True) + 1e-06) * gain


def project_kernel(scale, low, count, place_ref, normed_ref, own_ref, mine_ref, other_ref, out_ref, weight):
    me, core = place_ref[0], place_ref[1]
    row = lambda section, half: pl.ds(pl.multiple_of(section * 320 + half * 160, 16), 160)
    for t in range(count):
        weight[t, pl.ds(pl.multiple_of(me * 320, 16), 320), :] = own_ref[low + t]
        for source, half in ((mine_ref, core), (other_ref, 1 - core)):
            for k in range(3):
                section = lax.rem(me + k + 1, SECTIONS)
                weight[t, row(section, half), :] = source[k, t]
        made = jnp.dot(normed_ref[...], weight[t], preferred_element_type=f32)
        turned = (made * scale).T.astype(bf16)
        for h in range(ZN):
            out_ref[h, t * HD : (t + 1) * HD, :] = turned[h * HD : (h + 1) * HD, :]


def fetch(weight, low, count, core, *beside):
    half = lax.dynamic_slice(weight, (low, core * 160, 0), (count, 160, weight.shape[2]))
    right, left, *beside = lax.optimization_barrier((section_shift(half, -1), section_shift(half, 1), *beside))
    opp_a, opp_b = section_shift(right[:, :80], -1), section_shift(left[:, 80:], 1)
    return jnp.stack([right, jnp.concatenate([opp_a, opp_b], axis=1), left]), *beside


def project(place, normed, weight, low, mine, scale):
    count = mine.shape[1]
    other = blk_swap(mine, 1)
    return call(
        functools.partial(project_kernel, scale, low, count),
        jax.ShapeDtypeStruct((ZN, count * HD, 256), bf16),
        [SMEM] + [VMEM] * 4,
        [pltpu.VMEM((count, 1280, 640), bf16)],
        flops=2 * 256 * 1280 * 640 * count,
        moved=count * 2 * 1280 * 640,
        name="project",
    )(place, normed, weight, mine, other)


def attention_kernel(bounds_ref, place_ref, qframe_ref, kframe_ref, q_ref, own, near, far, across, out_ref, keys, values, held):
    y, core = place_ref[2], place_ref[1]
    filler = (lax.broadcasted_iota(jnp.int32, (48, 256), 0) == 0).astype(f32).astype(bf16)
    frame = lax.broadcasted_iota(jnp.int32, (16, 256), 0)

    def arrange(z, unused):
        for which, source in enumerate((own, near, far, across)):
            y_of = jnp.bitwise_xor(y, which // 2)
            core_of = jnp.bitwise_xor(core, which % 2)
            place = pl.ds(pl.multiple_of((y_of * 16 + z * 2 + core_of) * 256, 256), 256)
            keys[:HD, place] = source[z, :HD, :]
            other = (frame < 4) & (frame != kframe_ref[:, place])
            keys[HD:, place] = jnp.where(other, -1e30, 0.0).astype(bf16)
            values[place, :] = jnp.concatenate([source[z, HD:, :], filler], axis=0).T
        return unused

    lax.fori_loop(0, ZN, arrange, 0)

    def one_block(block, unused):
        tag = (frame == qframe_ref[pl.ds(block, 1), :]).astype(f32).astype(bf16)
        query = jnp.concatenate([q_ref[block], tag], axis=0).T
        first, last = bounds_ref[0, block], bounds_ref[1, block]

        def part(index):
            return pl.ds(pl.multiple_of(index * KB, KB), KB)

        def scores_of(index):
            return jnp.dot(query, keys[:, part(index)], preferred_element_type=f32)

        def absorb(scores, index, carry):
            top, accum = carry
            new_top = jnp.maximum(top, jnp.max(scores, axis=1, keepdims=True))
            weights = jnp.exp2(scores - new_top).astype(bf16)
            product = jnp.dot(weights, values[part(index), :], preferred_element_type=f32)
            return new_top, accum * jnp.exp2(top - new_top) + product

        def run(length, start, count, carry):
            def body(step, carry):
                index = start + length * step
                for k in range(length):
                    scores = held[k % 2]
                    held[(k + 1) % 2] = scores_of(jnp.minimum(index + k + 1, last - 1))
                    carry = absorb(scores, index + k, carry)
                return carry

            return lax.fori_loop(0, count, body, carry)

        held[0] = scores_of(first)
        carry = (jnp.full((256, 1), -1e30, f32), jnp.zeros((256, 128), f32))
        fours = (last - first) // 4
        carry = run(4, first, fours, carry)
        rest = first + 4 * fours
        twos = (last - rest) // 2
        carry = run(2, rest, twos, carry)
        carry = lax.fori_loop(rest + 2 * twos, last, lambda index, c: absorb(held[0], index, c), carry)
        accum = carry[1]
        result = accum / accum[:, HD : HD + 1]
        out_ref[block] = result.T[:HD, :].astype(bf16)
        return unused

    lax.fori_loop(0, ZN, one_block, 0)


def attention(place, frames, q, sources, y, core):
    ends = jnp.sum((frames[None, :] <= jnp.arange(-1, 4)[:, None]).astype(jnp.int32), axis=1)
    grid = frames.reshape(2, ZN, 2, 256)
    mine = lax.dynamic_index_in_dim(lax.dynamic_index_in_dim(grid, y, 0, False), core, 1, False)
    start, stop = ends[mine[:, 0]], ends[mine[:, -1] + 1]
    bounds = jnp.stack([start // KB, (stop + KB - 1) // KB]).astype(jnp.int32)
    return call(
        attention_kernel,
        jax.ShapeDtypeStruct((ZN, HD, 256), bf16),
        [SMEM, SMEM] + [VMEM] * 7,
        [pltpu.VMEM((HD + 16, 8192), bf16), pltpu.VMEM((8192, 128), bf16), pltpu.VMEM((2, 256, KB), f32)],
        flops=4 * 2048 * 4096 * 256,
        moved=4 * 8192 * HD,
        name="attention",
    )(bounds, place, mine, frames[None, :], q, *sources)


def output_kernel(
    place_ref, order_ref, gain_ref, patch_ref, attn_ref, attn_t_ref, own, right, left, opp_a, opp_b, out_ref, blocks
):
    me = place_ref[0]
    pick = (order_ref[...] == lax.broadcasted_iota(jnp.int32, (256, 256), 1)).astype(f32).astype(bf16)
    picked = []
    for source in (attn_ref, attn_t_ref):
        attn = source[...].reshape(ZN * HD, 256)
        chosen = lax.dot_general(pick, attn, (((1,), (1,)), ((), ())), preferred_element_type=f32)
        picked.append(chosen.astype(bf16))

    def product(weight, low, high):
        return sum(jnp.dot(picked[t][:, low:high], weight[t], preferred_element_type=f32) for t in range(2))

    blocks[me] = product(own, 0, 640)
    blocks[lax.rem(me + 1, SECTIONS)] = product(right, 0, 640)
    blocks[lax.rem(me + 3, SECTIONS)] = product(left, 0, 640)
    blocks[lax.rem(me + 2, SECTIONS)] = product(opp_a, 0, 320) + product(opp_b, 320, 640)
    total = jnp.dot(pick, patch_ref[...], preferred_element_type=f32)
    total += jnp.concatenate([blocks[section] for section in range(SECTIONS)], axis=1)
    out_ref[...] = rms_norm(total, gain_ref[...]).astype(bf16)


def merger_kernel(sizes, place_ref, *refs):
    count = len(sizes)
    sources, (up_ref, down_ref), outs, tokens = refs[:count], refs[count : count + 2], refs[count + 2 : -1], refs[-1]
    tp = place_ref[3]
    place = 0
    for source, size in zip(sources, sizes):
        for part in range(size // 128):
            half = jnp.bitwise_xor(tp, place % 2)
            rows = pl.ds(pl.multiple_of(place // 2 * 64 + half * 32, 32), 32)
            for j in range(4):
                low = part * 128 + j * 32
                tokens[j, rows, :] = source[low : low + 32, :]
            place += 1
    hidden = jnp.zeros((place * 32, 320), f32)
    for j in range(4):
        hidden += jnp.dot(tokens[j], up_ref[j * 1280 : (j + 1) * 1280, :], preferred_element_type=f32)
    hidden = (0.5 * hidden * (1.0 + lax.erf(hidden * (0.5**0.5)))).astype(bf16)
    for k in range(7):
        columns = slice(k * 512, (k + 1) * 512)
        made = jnp.dot(hidden, down_ref[:, columns], preferred_element_type=f32).astype(bf16)
        for n, out in enumerate(outs):
            out[:, columns] = made[n * 32 : (n + 1) * 32]


def merge(place, pieces, merger_up, merger_down, name):
    sizes = [piece.shape[0] for piece in pieces]
    total = sum(sizes) // 4
    return call(
        functools.partial(merger_kernel, sizes),
        tuple(jax.ShapeDtypeStruct((32, 3584), bf16) for _ in range(total // 32)),
        [SMEM] + [VMEM] * (len(pieces) + 2),
        [pltpu.VMEM((4, total, 1280), bf16)],
        flops=2 * 256 * 320 * (5120 + 3584),
        moved=6000000,
        name=name,
    )(place, *pieces, merger_up, merger_down)


def add(one, two):
    return (one.astype(f32) + two.astype(f32)).astype(bf16)


def send(value, distance, flip):
    route = [(s * 2 + t, (s + distance) % SECTIONS * 2 + (t ^ flip)) for s in range(SECTIONS) for t in range(2)]
    return lax.ppermute(value, ("section", "tp"), route)


def on_device(patches, frame_ids, groups, norm_gain, qkv_weight, out_weight, merge_gain, merger_up, merger_down):
    me, blk, tp = lax.axis_index("section"), lax.axis_index("blk"), lax.axis_index("tp")
    core, y = blk % 2, blk // 16
    place = jnp.stack([me, core, y, tp]).astype(jnp.int32)
    patch = patches[0]
    normed = rms_norm(patch.astype(f32), norm_gain).astype(bf16)

    out_half = tp_swap(lax.dynamic_slice_in_dim(out_weight, core * 160, 160, axis=1))
    kv_mine, out_half = fetch(qkv_weight, 1, 2, core, out_half)
    kv_mine, later = lax.optimization_barrier((kv_mine, qkv_weight))
    kv = z_exchange(project(place, normed, qkv_weight, 1, kv_mine, 1.0))
    out_rest = blk_swap(out_half, 1)
    out_weight_t = jnp.where(
        core == 0, jnp.concatenate([out_half, out_rest], axis=1), jnp.concatenate([out_rest, out_half], axis=1)
    )
    (q_mine,) = fetch(later, 0, 1, core)
    q_mine, out_own = lax.optimization_barrier((q_mine, jnp.stack([out_weight, out_weight_t])))
    out_right, out_left = section_shift(out_own, -1), section_shift(out_own, 1)
    q = project(place, normed, qkv_weight, 0, q_mine, HD ** (-0.5) * math.log2(math.e))
    kv, q = lax.optimization_barrier((kv, q))
    far = blk_swap(kv, 16)
    near = blk_swap(kv, 1)
    q = z_exchange(q)
    far, q, out_right, out_left = lax.optimization_barrier((far, q, out_right, out_left))
    across = blk_swap(far, 1)
    out_a, out_b = section_shift(out_right[:, :320], -1), section_shift(out_left[:, 320:], 1)

    attn = z_exchange(attention(place, frame_ids[0], q, (kv, near, far, across), y, core))
    attn_t = tp_swap(attn)
    order = groups[0].reshape(2, 32, 4).transpose(0, 2, 1).reshape(256, 1)
    own = call(
        output_kernel,
        jax.ShapeDtypeStruct((256, 1280), bf16),
        [SMEM] + [VMEM] * 10,
        [pltpu.VMEM((SECTIONS, 256, 320), f32)],
        flops=2 * 256 * 1280 * 1800,
        moved=5000000,
        name="output",
    )(place, order, merge_gain[None, :], patch, attn, attn_t, out_own, out_right, out_left, out_a, out_b)

    right, left = section_shift(own, -1), section_shift(own, 1)
    own_same, own_other = merge(place, [own], merger_up, merger_down, "merge_own")
    right, left, own_same, own_other = lax.optimization_barrier((right, left, own_same, own_other))
    opp_a, opp_b = section_shift(right[:128], -1), section_shift(left[128:], 1)
    mine = add(own_same, tp_swap(own_other))
    right_same, right_other, left_same, left_other = merge(
        place, [right, left], merger_up, merger_down, "merge_next"
    )
    opp_a, opp_b, right_other = lax.optimization_barrier((opp_a, opp_b, right_other))
    theirs = add(right_same, tp_swap(right_other))
    opp_same, opp_other = merge(place, [opp_a, opp_b], merger_up, merger_down, "merge_opposite")
    opp_same, opp_other, left_other, mine = lax.optimization_barrier((opp_same, opp_other, left_other, mine))
    sums = [send(opp_same, 3, 0), send(opp_other, 3, 1), section_shift(theirs, 2), section_shift(mine, 1)]
    sums += [left_same, tp_swap(left_other)]
    return sum(part.astype(f32) for part in sums).astype(bf16)[None]


def solution(mesh):
    in_specs = (
        P("section", "blk", None),
        P("section", None),
        P("section", "blk", None),
        P(),
        P(None, "section", "tp"),
        P("tp", "section"),
        P(),
        P(None, ("section", "tp")),
        P(("section", "tp"), None),
    )
    out_specs = P("section", ("blk", "tp"), None)
    return jax.shard_map(on_device, mesh=mesh, in_specs=in_specs, out_specs=out_specs, check_vma=False)
```

```python
import functools
import math

import jax
import jax.numpy as jnp
from jax import lax
from jax.experimental import pallas as pl
from jax.experimental.pallas import tpu as pltpu
from jax.sharding import PartitionSpec as P

HD = 80
ZN = 8
KB = 512
SECTIONS = 4
VMEM = pl.BlockSpec(memory_space=pltpu.VMEM)
SMEM = pl.BlockSpec(memory_space=pltpu.SMEM)
MIB = 1024 * 1024
bf16, f32 = jnp.bfloat16, jnp.float32

Z_GROUPS = [[y * 16 + z * 2 + c for z in range(ZN)] for y in range(2) for c in range(2)]


def call(kernel, out_shape, specs, scratch=(), flops=0, moved=0, name=None, grant=14):
    return pl.pallas_call(
        kernel,
        out_shape=out_shape,
        in_specs=specs,
        out_specs=jax.tree.map(lambda _: VMEM, out_shape),
        scratch_shapes=list(scratch),
        compiler_params=pltpu.CompilerParams(vmem_limit_bytes=grant * MIB),
        cost_estimate=pl.CostEstimate(flops=flops, bytes_accessed=moved, transcendentals=0),
        name=name,
    )


def section_shift(value, distance):
    route = [(i, (i + distance) % SECTIONS) for i in range(SECTIONS)]
    return lax.ppermute(value, "section", route)


def blk_swap(value, bit):
    return lax.ppermute(value, "blk", [(i, i ^ bit) for i in range(32)])


def tp_swap(value):
    return lax.ppermute(value, "tp", [(0, 1), (1, 0)])


def z_exchange(value):
    return lax.all_to_all(value, "blk", 0, 0, axis_index_groups=Z_GROUPS, tiled=True)


def rms_norm(value, gain):
    return value * lax.rsqrt(jnp.mean(value * value, axis=-1, keepdims=True) + 1e-06) * gain


def project_kernel(scale, low, count, place_ref, normed_ref, own_ref, mine_ref, other_ref, out_ref, weight):
    me, core = place_ref[0], place_ref[1]
    row = lambda section, half: pl.ds(pl.multiple_of(section * 320 + half * 160, 16), 160)
    for t in range(count):
        weight[t, pl.ds(pl.multiple_of(me * 320, 16), 320), :] = own_ref[low + t]
        for source, half in ((mine_ref, core), (other_ref, 1 - core)):
            for k in range(3):
                section = lax.rem(me + k + 1, SECTIONS)
                weight[t, row(section, half), :] = source[k, t]
        made = jnp.dot(normed_ref[...], weight[t], preferred_element_type=f32)
        turned = (made * scale).T.astype(bf16)
        for h in range(ZN):
            out_ref[h, t * HD : (t + 1) * HD, :] = turned[h * HD : (h + 1) * HD, :]


def fetch(weight, low, count, core, *beside):
    half = lax.dynamic_slice(weight, (low, core * 160, 0), (count, 160, weight.shape[2]))
    right, left, *beside = lax.optimization_barrier((section_shift(half, -1), section_shift(half, 1), *beside))
    opp_a, opp_b = section_shift(right[:, :80], -1), section_shift(left[:, 80:], 1)
    return jnp.stack([right, jnp.concatenate([opp_a, opp_b], axis=1), left]), *beside


def project(place, normed, weight, low, mine, scale):
    count = mine.shape[1]
    other = blk_swap(mine, 1)
    return call(
        functools.partial(project_kernel, scale, low, count),
        jax.ShapeDtypeStruct((ZN, count * HD, 256), bf16),
        [SMEM] + [VMEM] * 4,
        [pltpu.VMEM((count, 1280, 640), bf16)],
        flops=2 * 256 * 1280 * 640 * count,
        moved=count * 2 * 1280 * 640,
        name="project",
    )(place, normed, weight, mine, other)


def attention_kernel(bounds_ref, place_ref, qframe_ref, kframe_ref, q_ref, own, near, far, across, out_ref, keys, values, held):
    y, core = place_ref[2], place_ref[1]
    filler = (lax.broadcasted_iota(jnp.int32, (48, 256), 0) == 0).astype(f32).astype(bf16)
    frame = lax.broadcasted_iota(jnp.int32, (16, 256), 0)

    def arrange(z, unused):
        for which, source in enumerate((own, near, far, across)):
            y_of = jnp.bitwise_xor(y, which // 2)
            core_of = jnp.bitwise_xor(core, which % 2)
            place = pl.ds(pl.multiple_of((y_of * 16 + z * 2 + core_of) * 256, 256), 256)
            keys[:HD, place] = source[z, :HD, :]
            other = (frame < 4) & (frame != kframe_ref[:, place])
            keys[HD:, place] = jnp.where(other, -1e30, 0.0).astype(bf16)
            values[place, :] = jnp.concatenate([source[z, HD:, :], filler], axis=0).T
        return unused

    lax.fori_loop(0, ZN, arrange, 0)

    def one_block(block, unused):
        tag = (frame == qframe_ref[pl.ds(block, 1), :]).astype(f32).astype(bf16)
        query = jnp.concatenate([q_ref[block], tag], axis=0).T
        first, last = bounds_ref[0, block], bounds_ref[1, block]

        def part(index):
            return pl.ds(pl.multiple_of(index * KB, KB), KB)

        def scores_of(index):
            return jnp.dot(query, keys[:, part(index)], preferred_element_type=f32)

        def absorb(scores, index, carry):
            top, accum = carry
            new_top = jnp.maximum(top, jnp.max(scores, axis=1, keepdims=True))
            weights = jnp.exp2(scores - new_top).astype(bf16)
            product = jnp.dot(weights, values[part(index), :], preferred_element_type=f32)
            return new_top, accum * jnp.exp2(top - new_top) + product

        def run(length, start, count, carry):
            def body(step, carry):
                index = start + length * step
                for k in range(length):
                    scores = held[k % 2]
                    held[(k + 1) % 2] = scores_of(jnp.minimum(index + k + 1, last - 1))
                    carry = absorb(scores, index + k, carry)
                return carry

            return lax.fori_loop(0, count, body, carry)

        held[0] = scores_of(first)
        carry = (jnp.full((256, 1), -1e30, f32), jnp.zeros((256, 128), f32))
        rest = first
        for length in (8, 4, 2):
            count = (last - rest) // length
            carry = run(length, rest, count, carry)
            rest += length * count
        carry = lax.fori_loop(rest, last, lambda index, c: absorb(held[0], index, c), carry)
        accum = carry[1]
        result = accum / accum[:, HD : HD + 1]
        out_ref[block] = result.T[:HD, :].astype(bf16)
        return unused

    lax.fori_loop(0, ZN, one_block, 0)


def attention(place, frames, q, sources, y, core):
    ends = jnp.sum((frames[None, :] <= jnp.arange(-1, 4)[:, None]).astype(jnp.int32), axis=1)
    grid = frames.reshape(2, ZN, 2, 256)
    mine = lax.dynamic_index_in_dim(lax.dynamic_index_in_dim(grid, y, 0, False), core, 1, False)
    start, stop = ends[mine[:, 0]], ends[mine[:, -1] + 1]
    bounds = jnp.stack([start // KB, (stop + KB - 1) // KB]).astype(jnp.int32)
    return call(
        attention_kernel,
        jax.ShapeDtypeStruct((ZN, HD, 256), bf16),
        [SMEM, SMEM] + [VMEM] * 7,
        [pltpu.VMEM((HD + 16, 8192), bf16), pltpu.VMEM((8192, 128), bf16), pltpu.VMEM((2, 256, KB), f32)],
        flops=4 * 2048 * 4096 * 256,
        moved=4 * 8192 * HD,
        name="attention",
    )(bounds, place, mine, frames[None, :], q, *sources)


def output_kernel(
    place_ref, order_ref, gain_ref, patch_ref, attn_ref, attn_t_ref, own, right, left, opp_a, opp_b, out_ref, blocks
):
    me = place_ref[0]
    pick = (order_ref[...] == lax.broadcasted_iota(jnp.int32, (256, 256), 1)).astype(f32).astype(bf16)
    picked = []
    for source in (attn_ref, attn_t_ref):
        attn = source[...].reshape(ZN * HD, 256)
        chosen = lax.dot_general(pick, attn, (((1,), (1,)), ((), ())), preferred_element_type=f32)
        picked.append(chosen.astype(bf16))

    def product(weight, low, high):
        return sum(jnp.dot(picked[t][:, low:high], weight[t], preferred_element_type=f32) for t in range(2))

    blocks[me] = product(own, 0, 640)
    blocks[lax.rem(me + 1, SECTIONS)] = product(right, 0, 640)
    blocks[lax.rem(me + 3, SECTIONS)] = product(left, 0, 640)
    blocks[lax.rem(me + 2, SECTIONS)] = product(opp_a, 0, 320) + product(opp_b, 320, 640)
    total = jnp.dot(pick, patch_ref[...], preferred_element_type=f32)
    total += jnp.concatenate([blocks[section] for section in range(SECTIONS)], axis=1)
    out_ref[...] = rms_norm(total, gain_ref[...]).astype(bf16)


def merger_kernel(sizes, place_ref, *refs):
    count = len(sizes)
    sources, (up_ref, down_ref), outs, tokens = refs[:count], refs[count : count + 2], refs[count + 2 : -1], refs[-1]
    tp = place_ref[3]
    place = 0
    for source, size in zip(sources, sizes):
        for part in range(size // 128):
            half = jnp.bitwise_xor(tp, place % 2)
            rows = pl.ds(pl.multiple_of(place // 2 * 64 + half * 32, 32), 32)
            for j in range(4):
                low = part * 128 + j * 32
                tokens[j, rows, :] = source[low : low + 32, :]
            place += 1
    hidden = jnp.zeros((place * 32, 320), f32)
    for j in range(4):
        hidden += jnp.dot(tokens[j], up_ref[j * 1280 : (j + 1) * 1280, :], preferred_element_type=f32)
    hidden = (0.5 * hidden * (1.0 + lax.erf(hidden * (0.5**0.5)))).astype(bf16)
    for k in range(7):
        columns = slice(k * 512, (k + 1) * 512)
        made = jnp.dot(hidden, down_ref[:, columns], preferred_element_type=f32).astype(bf16)
        for n, out in enumerate(outs):
            out[:, columns] = made[n * 32 : (n + 1) * 32]


def merge(place, pieces, merger_up, merger_down, name):
    sizes = [piece.shape[0] for piece in pieces]
    total = sum(sizes) // 4
    return call(
        functools.partial(merger_kernel, sizes),
        tuple(jax.ShapeDtypeStruct((32, 3584), bf16) for _ in range(total // 32)),
        [SMEM] + [VMEM] * (len(pieces) + 2),
        [pltpu.VMEM((4, total, 1280), bf16)],
        flops=2 * 256 * 320 * (5120 + 3584),
        moved=6000000,
        name=name,
    )(place, *pieces, merger_up, merger_down)


def add(one, two):
    return (one.astype(f32) + two.astype(f32)).astype(bf16)


def send(value, distance, flip):
    route = [(s * 2 + t, (s + distance) % SECTIONS * 2 + (t ^ flip)) for s in range(SECTIONS) for t in range(2)]
    return lax.ppermute(value, ("section", "tp"), route)


def on_device(patches, frame_ids, groups, norm_gain, qkv_weight, out_weight, merge_gain, merger_up, merger_down):
    me, blk, tp = lax.axis_index("section"), lax.axis_index("blk"), lax.axis_index("tp")
    core, y = blk % 2, blk // 16
    place = jnp.stack([me, core, y, tp]).astype(jnp.int32)
    patch = patches[0]
    normed = rms_norm(patch.astype(f32), norm_gain).astype(bf16)

    out_half = tp_swap(lax.dynamic_slice_in_dim(out_weight, core * 160, 160, axis=1))
    kv_mine, out_half = fetch(qkv_weight, 1, 2, core, out_half)
    kv_mine, later = lax.optimization_barrier((kv_mine, qkv_weight))
    kv = z_exchange(project(place, normed, qkv_weight, 1, kv_mine, 1.0))
    out_rest = blk_swap(out_half, 1)
    out_weight_t = jnp.where(
        core == 0, jnp.concatenate([out_half, out_rest], axis=1), jnp.concatenate([out_rest, out_half], axis=1)
    )
    (q_mine,) = fetch(later, 0, 1, core)
    q_mine, out_own = lax.optimization_barrier((q_mine, jnp.stack([out_weight, out_weight_t])))
    out_right, out_left = section_shift(out_own, -1), section_shift(out_own, 1)
    q = project(place, normed, qkv_weight, 0, q_mine, HD ** (-0.5) * math.log2(math.e))
    kv, q = lax.optimization_barrier((kv, q))
    far = blk_swap(kv, 16)
    near = blk_swap(kv, 1)
    q = z_exchange(q)
    far, q, out_right, out_left = lax.optimization_barrier((far, q, out_right, out_left))
    across = blk_swap(far, 1)
    out_a, out_b = section_shift(out_right[:, :320], -1), section_shift(out_left[:, 320:], 1)

    attn = z_exchange(attention(place, frame_ids[0], q, (kv, near, far, across), y, core))
    attn_t = tp_swap(attn)
    order = groups[0].reshape(2, 32, 4).transpose(0, 2, 1).reshape(256, 1)
    own = call(
        output_kernel,
        jax.ShapeDtypeStruct((256, 1280), bf16),
        [SMEM] + [VMEM] * 10,
        [pltpu.VMEM((SECTIONS, 256, 320), f32)],
        flops=2 * 256 * 1280 * 1800,
        moved=5000000,
        name="output",
    )(place, order, merge_gain[None, :], patch, attn, attn_t, out_own, out_right, out_left, out_a, out_b)

    right, left = section_shift(own, -1), section_shift(own, 1)
    own_same, own_other = merge(place, [own], merger_up, merger_down, "merge_own")
    right, left, own_same, own_other = lax.optimization_barrier((right, left, own_same, own_other))
    opp_a, opp_b = section_shift(right[:128], -1), section_shift(left[128:], 1)
    mine = add(own_same, tp_swap(own_other))
    right_same, right_other, left_same, left_other = merge(
        place, [right, left], merger_up, merger_down, "merge_next"
    )
    opp_a, opp_b, right_other = lax.optimization_barrier((opp_a, opp_b, right_other))
    theirs = add(right_same, tp_swap(right_other))
    opp_same, opp_other = merge(place, [opp_a, opp_b], merger_up, merger_down, "merge_opposite")
    opp_same, opp_other, left_other, mine = lax.optimization_barrier((opp_same, opp_other, left_other, mine))
    sums = [send(opp_same, 3, 0), send(opp_other, 3, 1), section_shift(theirs, 2), section_shift(mine, 1)]
    sums += [left_same, tp_swap(left_other)]
    return sum(part.astype(f32) for part in sums).astype(bf16)[None]


def solution(mesh):
    in_specs = (
        P("section", "blk", None),
        P("section", None),
        P("section", "blk", None),
        P(),
        P(None, "section", "tp"),
        P("tp", "section"),
        P(),
        P(None, ("section", "tp")),
        P(("section", "tp"), None),
    )
    out_specs = P("section", ("blk", "tp"), None)
    return jax.shard_map(on_device, mesh=mesh, in_specs=in_specs, out_specs=out_specs, check_vma=False)
```
